512 devices in a mesh: gy: 32 (over y_lo, z), gz: 16 (over y_hi, x, core).
Axes of the slice: x: 4, y: 4 (y_hi: 2, y_lo: 2; y = y_hi * 2 + y_lo), z: 16, core: 2. Of those that a mesh axis runs over, the one named last changes fastest.
Arguments:
- field: bfloat16 [20, 64, 64, 2048], P(None, 'gy', 'gz'), may hold values from -6 to 6
- cotangent: bfloat16 [20, 64, 64, 2048], P(None, 'gy', 'gz'), may hold values from -6 to 6
- spectral_weight: bfloat16 [576, 230400], P('gz', 'gy'), may hold values from -3 to 3
- point_weight: bfloat16 [20, 20], replicated, may hold values from -1.25 to 1.25
- channel_bias: float32 [20], replicated, may hold values from -3 to 3
Outputs:
- layer_output: bfloat16 [20, 64, 64, 2048], P(None, 'gy', 'gz')
- field_grad: bfloat16 [20, 64, 64, 2048], P(None, 'gy', 'gz')
- weight_grad: float32 [576, 230400], P('gz', 'gy')
The draws below stay inside these ranges and needn't reach their ends.
All inputs are finite; a program needn't handle non-finite values.
Results may differ from the reference program's by a relative error of at most 0.02.
Values may be sent and summed in bfloat16 or wider, within the bound.
A program may use at most 128 MiB of HBM per device.

```python
import jax
import jax.numpy as jnp
from jax import lax

CH = 20
MODES = 12
NX = 64
NY = 64
NZ = 64
NT = 32
NKXT = 288
NKYZ = 576


def block_scale(own_key, extent, split, low, high):
    def one(dim, parts):
        steps = jax.random.uniform(jax.random.fold_in(jax.random.fold_in(own_key, 6), dim), (parts,), jnp.float32, low / len(split), high / len(split))
        return jnp.repeat(jnp.exp(steps), extent[dim] // parts).reshape((-1,) + (1,) * (len(extent) - dim - 1))

    loudness = one(*split[0])
    for cut in split[1:]:
        loudness = loudness * one(*cut)
    return loudness


def scatter_about(stream_key, shape, width, reach, split=(), held_as=jnp.bfloat16):
    array = jax.random.normal(stream_key, shape, jnp.float32) * width
    if len(split) > 0:
        array = block_scale(stream_key, shape, split, -0.22, 0.18) * array
    return jnp.clip(array, min=-reach, max=reach).astype(held_as)


def setup_inputs(seed: int = 0) -> dict:
    splits = jax.random.split(jax.random.key(seed), 6)
    field = scatter_about(splits[0], (CH, NY, NZ, NX * NT), 1.0, 6.0, ((1, 32), (2, 16)))
    cotangent = scatter_about(splits[1], (CH, NY, NZ, NX * NT), 1.0, 6.0, ((1, 32), (2, 16)))
    spectral_weight = scatter_about(splits[2], (NKYZ, NKXT * 2 * CH * CH), 0.5, 3.0, ((0, 16), (1, 32)))
    point_weight = scatter_about(splits[3], (CH, CH), CH ** -0.5, 1.25)
    channel_bias = scatter_about(splits[4], (CH,), 0.5, 3.0, (), jnp.float32)
    return {"field": field, "cotangent": cotangent, "spectral_weight": spectral_weight, "point_weight": point_weight, "channel_bias": channel_bias}


def kept_frequency(length):
    slots = jnp.arange(2 * MODES, dtype=jnp.int32)
    return jnp.where(slots < MODES, slots, length - 2 * MODES + slots).astype(jnp.int32)


def analyse_planes(values):
    def per_channel(plane):
        volume = plane.astype(jnp.float32).reshape(NY, NZ, NX, NT)
        spectrum = jnp.fft.rfft(volume, axis=3)[..., :MODES]
        spectrum = jnp.fft.fft(spectrum, axis=2)
        spectrum = jnp.take(spectrum, kept_frequency(NX), axis=2)
        stacked = jnp.stack([spectrum.real, spectrum.imag], axis=-1)
        return stacked.reshape(NY, NZ, NKXT * 2).astype(jnp.bfloat16)
    return lax.map(per_channel, values)


def analyse_pencils(values):
    def per_channel(plane):
        pairs = plane.astype(jnp.float32).reshape(NY, NZ, NKXT, 2)
        complex_values = pairs[..., 0] + 1j * pairs[..., 1]
        spectrum = jnp.fft.fft(jnp.fft.fft(complex_values, axis=0), axis=1)
        spectrum = jnp.take(spectrum, kept_frequency(NY), axis=0)
        spectrum = jnp.take(spectrum, kept_frequency(NZ), axis=1)
        spectrum = spectrum.reshape(NKYZ, NKXT)
        return jnp.stack([spectrum.real, spectrum.imag], axis=-1)
    return jnp.transpose(lax.map(per_channel, values), (1, 2, 3, 0))


def synthesise_pencils(coeffs):
    def per_channel(block):
        values = block.astype(jnp.float32)
        complex_values = (values[..., 0] + 1j * values[..., 1]).reshape(2 * MODES, 2 * MODES, NKXT)
        padded = jnp.zeros((NY, NZ, NKXT), complex_values.dtype)
        padded = padded.at[kept_frequency(NY)[:, None], kept_frequency(NZ)[None, :]].set(complex_values)
        planes = jnp.fft.ifft(jnp.fft.ifft(padded, axis=0), axis=1) * (NY * NZ)
        stacked = jnp.stack([planes.real, planes.imag], axis=-1)
        return stacked.reshape(NY, NZ, NKXT * 2).astype(jnp.bfloat16)
    return lax.map(per_channel, jnp.transpose(coeffs, (3, 0, 1, 2)))


def synthesise_planes(values):
    def per_channel(plane):
        pairs = plane.astype(jnp.float32).reshape(NY, NZ, 2 * MODES, MODES, 2)
        complex_values = pairs[..., 0] + 1j * pairs[..., 1]
        padded = jnp.zeros((NY, NZ, NX, NT), complex_values.dtype)
        time_slots = jnp.arange(MODES, dtype=jnp.int32)
        padded = padded.at[:, :, kept_frequency(NX)[:, None], time_slots[None, :]].set(complex_values)
        volume = jnp.fft.ifft(jnp.fft.ifft(padded, axis=2), axis=3) * (NX * NT)
        return volume.real.reshape(NY, NZ, NX * NT)
    return lax.map(per_channel, values)


def mode_scale():
    time_slot = jnp.arange(NKXT, dtype=jnp.int32) % MODES
    return jnp.where(time_slot == 0, 1.0, 2.0).astype(jnp.float32) / (NX * NY * NZ * NT)


def reference(field, cotangent, spectral_weight, point_weight, channel_bias):
    highest = lax.Precision.HIGHEST
    scaling = mode_scale()[None, :, None, None]
    coeffs = analyse_pencils(analyse_planes(field))
    kernel = spectral_weight.astype(jnp.float32).reshape(NKYZ, NKXT, 2, CH, CH)
    real_in, imag_in = coeffs[:, :, 0], coeffs[:, :, 1]
    real_w, imag_w = kernel[:, :, 0], kernel[:, :, 1]
    real_part = jnp.einsum("pqi,pqio->pqo", real_in, real_w, precision=highest) - jnp.einsum("pqi,pqio->pqo", imag_in, imag_w, precision=highest)
    imag_part = jnp.einsum("pqi,pqio->pqo", real_in, imag_w, precision=highest) + jnp.einsum("pqi,pqio->pqo", imag_in, real_w, precision=highest)
    spectrum = (jnp.stack([real_part, imag_part], axis=2) * scaling).astype(jnp.bfloat16)
    spectral_out = synthesise_planes(synthesise_pencils(spectrum))
    mixing = point_weight.astype(jnp.float32)
    preact = spectral_out + jnp.einsum("io,iyzr->oyzr", mixing, field.astype(jnp.float32), precision=highest) + channel_bias[:, None, None, None]
    normal_cdf = 0.5 * (1.0 + lax.erf(preact * 0.7071067811865476))
    density = jnp.exp(-0.5 * preact * preact) * 0.3989422804014327
    layer_output = (preact * normal_cdf).astype(jnp.bfloat16)
    slope_grad = (cotangent.astype(jnp.float32) * (normal_cdf + preact * density)).astype(jnp.bfloat16)
    grads = analyse_pencils(analyse_planes(slope_grad)) * scaling
    real_g, imag_g = grads[:, :, 0], grads[:, :, 1]
    grad_real = jnp.einsum("pqi,pqo->pqio", real_in, real_g, precision=highest) + jnp.einsum("pqi,pqo->pqio", imag_in, imag_g, precision=highest)
    grad_imag = jnp.einsum("pqi,pqo->pqio", real_in, imag_g, precision=highest) - jnp.einsum("pqi,pqo->pqio", imag_in, real_g, precision=highest)
    weight_grad = jnp.stack([grad_real, grad_imag], axis=2).reshape(NKYZ, NKXT * 2 * CH * CH)
    back_real = jnp.einsum("pqio,pqo->pqi", real_w, real_g, precision=highest) + jnp.einsum("pqio,pqo->pqi", imag_w, imag_g, precision=highest)
    back_imag = jnp.einsum("pqio,pqo->pqi", real_w, imag_g, precision=highest) - jnp.einsum("pqio,pqo->pqi", imag_w, real_g, precision=highest)
    mode_back = jnp.stack([back_real, back_imag], axis=2).astype(jnp.bfloat16)
    spectral_back = synthesise_planes(synthesise_pencils(mode_back))
    field_grad = (spectral_back + jnp.einsum("io,oyzr->iyzr", mixing, slope_grad.astype(jnp.float32), precision=highest)).astype(jnp.bfloat16)
    return layer_output, field_grad, weight_grad
```

```python
import functools

import jax
import jax.numpy as jnp
import ml_dtypes
import numpy as np
from jax import lax
from jax.experimental import pallas as pl
from jax.experimental.pallas import tpu as pltpu
from jax.sharding import PartitionSpec as P

MODES = 12
NX = 64
NY = 64
NZ = 64
NT = 32
CH = 20
GY = 32
GZ = 16
PAIRS = 36
PROWS = 40
SLAB = 24
MESH = pl.DeviceIdType.MESH
BF = jnp.bfloat16
F32 = jnp.float32


def kept(slots, length):
    return np.where(slots < MODES, slots, length - 2 * MODES + slots)


def plane_constant():
    cell = np.arange(NX * NT)
    x, t = cell // NT, cell % NT
    out = np.zeros((GY, 3, 8, NX * NT))
    for d in range(GY):
        for k in range(3):
            for q3 in range(3):
                q = 9 * d + 3 * k + q3
                kx, kt = kept(np.array(q // MODES), NX), q % MODES
                angle = 2 * np.pi * ((kx * x % NX) / NX + (kt * t % NT) / NT)
                out[d, k, 2 * q3] = np.cos(angle)
                out[d, k, 2 * q3 + 1] = -np.sin(angle)
    return out.reshape(GY * SLAB, NX * NT)


def slot_frequency(length):
    g = np.arange(GZ)[:, None]
    return kept(3 * g // 2 + np.arange(2)[None, :], length)


def on_slabs(cosine, sine):
    rows, cols = cosine.shape
    two = np.stack([np.stack([cosine, sine], -1), np.stack([-sine, cosine], -1)], 2)
    full = np.einsum("rcab,uv->ruacvb", two.transpose(0, 1, 2, 3), np.eye(12))
    return full.reshape(rows * SLAB, cols * SLAB)


def y_constants():
    ky = slot_frequency(NY)
    y = 2 * np.arange(GY)[None, :] + np.arange(2)[:, None]
    angle = 2 * np.pi * (ky[None, :, :, None] * y[:, None, None, :] % NY) / NY
    near = angle.transpose(0, 2, 1, 3)
    forward = on_slabs(np.cos(near).reshape(-1, GY), np.sin(near).reshape(-1, GY))
    far = angle.transpose(0, 2, 3, 1)
    back = on_slabs(np.cos(far).reshape(-1, GZ), -np.sin(far).reshape(-1, GZ))
    return forward, back


def pair_slots(parity):
    p = np.arange(PAIRS) + 12 * parity
    return p // 24, p % 24


def z_constants():
    forward = np.zeros((2, 4, 2, 3, 168, GZ, 12, 2))
    back = np.zeros((2, 4, GZ, 12, 2, 2, 3, 168))
    for parity in range(2):
        kz = kept(pair_slots(parity)[1], NZ)
        for zl in range(4):
            angle = 2 * np.pi * (kz[:, None] * (4 * np.arange(GZ) + zl)[None, :] % NZ) / NZ
            c, s = np.cos(angle), np.sin(angle)
            for k in range(3):
                for q3 in range(4):
                    rows = slice(PROWS * q3, PROWS * q3 + PAIRS) if q3 < 3 else slice(128, 128 + PAIRS)
                    u = 4 * k + q3
                    forward[parity, zl, 0, k, rows, :, u, 0] = c
                    forward[parity, zl, 0, k, rows, :, u, 1] = s
                    forward[parity, zl, 1, k, rows, :, u, 0] = -s
                    forward[parity, zl, 1, k, rows, :, u, 1] = c
                    back[parity, zl, :, u, 0, 0, k, rows] = c.T
                    back[parity, zl, :, u, 0, 1, k, rows] = -s.T
                    back[parity, zl, :, u, 1, 0, k, rows] = s.T
                    back[parity, zl, :, u, 1, 1, k, rows] = c.T
    back = np.pad(back.reshape(2, 4 * GZ * SLAB, 1008), ((0, 0), (0, 0), (0, 16)))
    return forward.reshape(2, 4 * 1008, GZ * SLAB), back


def mask_constant():
    lane = np.arange(128)
    out = np.zeros((2, 2, 128, 128))
    for parity in range(2):
        slot = pair_slots(parity)[0]
        for q3 in range(3):
            rows = slice(PROWS * q3, PROWS * q3 + PAIRS)
            match = (lane // 4 % 2)[None, :] == slot[:, None]
            out[parity, 0, rows] = match
            out[parity, 1, rows] = match & (lane // 32 == q3)[None, :]
    return out


def channel_constants():
    lane = np.arange(128)
    channel = np.concatenate([lane // 8, np.where(lane < 96, 16 + lane % 32 // 8, -1)])
    pair = np.arange(512)
    first = np.where(pair < CH * CH, pair // CH, -2)
    second = np.where(pair < CH * CH, pair % CH, -2)
    return channel[:, None] == first[None, :], channel[:, None] == second[None, :]


@functools.cache
def constants():
    half = lambda a: np.asarray(a, np.float32).astype(ml_dtypes.bfloat16)
    y_forward, y_back = y_constants()
    z_forward, z_back = z_constants()
    first, second = channel_constants()
    spread = np.stack([first, second])
    return (
        half(plane_constant()),
        half(y_forward),
        half(z_forward),
        half(z_back),
        half(y_back),
        half(spread),
        half(spread.transpose(0, 2, 1)),
        np.asarray(mask_constant(), np.float32),
    )


def dot(a, b):
    return jnp.dot(a, b, preferred_element_type=F32)


def dot_t(a, b):
    return lax.dot_general(a, b, (((1,), (1,)), ((), ())), preferred_element_type=F32)


def lanes(shape):
    return lax.broadcasted_iota(jnp.int32, shape, len(shape) - 1)


def kernel(
    field_hbm, cot_hbm, weight_hbm, point_ref, bias_ref,
    plane_hbm, yf_hbm, zf_hbm, zb_hbm, yb_hbm, spread_hbm, gather_hbm, mask_hbm,
    out_hbm, fgrad_hbm, wgrad_hbm,
    field, cot, weight, plane, yf, zf, zb, yb, spread, gather, mask,
    slope, layer, fgrad, wf, w0, w1, u0, u1, wg, wgrad, turned, scale, point_fwd, point_bwd, bias_col,
    sy, ry, sz, rz, szb, rzb, syb, ryb, load_sem, store_sem, send_sem, recv_sem,
):
    j = lax.axis_index("gy")
    g = lax.axis_index("gz")
    parity = lax.rem(g, 2)

    def load(i, src, dst):
        copy = pltpu.make_async_copy(src, dst, load_sem.at[i])
        copy.start()
        return copy

    got_field = load(0, field_hbm, field.at[pl.ds(0, 160)])
    got_plane = load(1, plane_hbm, plane)
    got_yf = load(2, yf_hbm, yf)
    got_weight = load(3, weight_hbm, weight)
    got_zf = load(4, zf_hbm.at[parity], zf)
    got_spread = load(5, spread_hbm, spread)
    got_gather = load(6, gather_hbm, gather)
    got_mask = load(7, mask_hbm.at[parity], mask)
    got_zb = load(8, zb_hbm.at[parity], zb)
    got_yb = load(9, yb_hbm, yb)
    got_cot = load(10, cot_hbm, cot)

    barrier = pltpu.get_barrier_semaphore()

    def greet(axis, me, count):
        def one(k, carry):
            pl.semaphore_signal(barrier, inc=1, device_id={axis: lax.rem(me + k, count)}, device_id_type=MESH)
            return carry

        lax.fori_loop(1, count, one, 0)

    greet("gy", j, GY)
    greet("gz", g, GZ)

    def send(src, dst, axis, me, count, which):
        def one(k, carry):
            other = lax.rem(me + k, count)
            pltpu.make_async_remote_copy(
                src_ref=src.at[other],
                dst_ref=dst.at[me],
                send_sem=send_sem.at[which],
                recv_sem=recv_sem.at[which],
                device_id={axis: other},
                device_id_type=MESH,
            ).start()
            return carry

        lax.fori_loop(1, count, one, 0)
        dst[pl.ds(me, 1)] = src[pl.ds(me, 1)]

    def arrive(src, dst, count, which):
        part = pl.ds(0, count - 1)
        pltpu.make_async_copy(dst.at[part], dst.at[part], recv_sem.at[which]).wait()
        pltpu.make_async_copy(src.at[part], src.at[part], send_sem.at[which]).wait()

    zlane = lanes((1, 128)) % 4
    low_slot = lanes((1, 128)) // 4 % 2 == 0
    row3 = lax.broadcasted_iota(jnp.int32, (1, 8, 128), 1)
    lane3 = lanes((1, 8, 128))

    def planes_out(source, buffer):
        full = dot_t(plane[...], source[...])
        main = full[:, :128].reshape(96, 8, 128)
        left = full[:, 128:].reshape(96, 8, 128)
        extra = jnp.zeros_like(main)
        for q3 in range(3):
            moved = pltpu.roll(left, 6 - 2 * q3, 1)
            if q3:
                moved = pltpu.roll(moved, 32 * q3, 2)
            extra = jnp.where(lane3 // 32 == q3, moved, extra)
        buffer[...] = jnp.where(row3 >= 6, extra, main).reshape(GY, SLAB, 128).astype(BF)

    def planes_in(buffer):
        block = buffer[...].astype(F32).reshape(96, 8, 128)
        left = jnp.zeros_like(block)
        for q3 in range(3):
            moved = pltpu.roll(block, 2 + 2 * q3, 1)
            if q3:
                moved = pltpu.roll(moved, 128 - 32 * q3, 2)
            left = jnp.where(row3 // 2 == q3, moved, left)
        turned[0:128] = block.reshape(768, 128).T.astype(BF)
        turned[128:256] = left.reshape(768, 128).T.astype(BF)

    def swap_slots(same_low, same_high, cross_low, cross_high):
        crossed = jnp.where(low_slot, pltpu.roll(cross_low, 124, 1), pltpu.roll(cross_high, 4, 1))
        return jnp.where(low_slot, same_low, same_high) + crossed

    def y_forward(buffer, target):
        block = buffer[...].reshape(768, 128)
        part = [dot(yf[384 * n : 384 * n + 384], block) for n in range(4)]
        target[...] = swap_slots(part[0], part[3], part[2], part[1]).reshape(GZ, SLAB, 128).astype(BF)

    def y_back(buffer, target):
        block = buffer[...].reshape(384, 128)
        part = [dot(yb[768 * n : 768 * n + 768], block) for n in range(4)]
        target[...] = swap_slots(part[0], part[3], part[1], part[2]).reshape(GY, SLAB, 128).astype(BF)

    def by_z(parts):
        low = jnp.where(zlane == 0, parts[0], parts[1])
        high = jnp.where(zlane == 2, parts[2], parts[3])
        return jnp.where(zlane < 2, low, high)

    def z_forward(buffer, factor):
        block = buffer[...].reshape(384, 128)
        values = by_z([dot(zf[1008 * n : 1008 * n + 1008], block) for n in range(4)]).reshape(6, 168, 128)
        left = values[:, 128:]
        left = jnp.concatenate([left, left, left, jnp.zeros((6, 8, 128), F32)], axis=1)
        main = (values[:, :128] * mask[0:1]).reshape(768, 128)
        left = (left * mask[1:2]).reshape(768, 128)
        if factor is not None:
            main, left = main * factor, left * factor
        return jnp.concatenate([main.astype(BF), left.astype(BF)], axis=1)

    def z_back(mixed, n, factor, target):
        values = dot(mixed, gather[n])
        if factor is not None:
            values = values * jnp.concatenate([factor, factor], axis=1)
        main = values[:, :128].reshape(6, 128, 128) * mask[0:1]
        left = values[:, 128:].reshape(6, 128, 128) * mask[1:2]
        left = left[:, 0:40] + left[:, 40:80] + left[:, 80:120]
        rows = jnp.concatenate([main, left], axis=1).reshape(1008, 128)
        rows = jnp.concatenate([rows, jnp.zeros((16, 128), F32)], axis=0).astype(BF)
        parts = [dot(zb[384 * n : 384 * n + 384], rows) for n in range(4)]
        target[...] = by_z(parts).reshape(GZ, SLAB, 128).astype(BF)

    field[160:256] = jnp.zeros((96, 2048), BF)
    slope[160:256] = jnp.zeros((96, 2048), BF)

    got_field.wait()
    got_plane.wait()
    planes_out(field, sy.at[0])
    pl.semaphore_wait(barrier, GY + GZ - 2)
    send(sy.at[0], ry.at[0], "gy", j, GY, 0)

    got_weight.wait()
    wf[...] = jnp.zeros((PROWS, 7296), F32)
    wf[0:PAIRS, 0:7200] = weight[...].astype(F32)
    w0[...] = jnp.zeros((384, 512), F32)
    w1[...] = jnp.zeros((384, 512), F32)
    for q in range(9):
        for part, held in enumerate((w0, w1)):
            start = 800 * q + 400 * part
            first, shift = start // 128 * 128, start % 128
            piece = wf[:, first : first + 512]
            if shift:
                piece = pltpu.roll(piece, 512 - shift, 1)
            top = 128 * (q // 3) + PROWS * (q % 3)
            held[top : top + PROWS] = piece
    row = lax.broadcasted_iota(jnp.int32, (384, 128), 0)
    inner = row % 128
    mode = 9 * j + 3 * (row // 128) + (inner >= 40).astype(jnp.int32) + (inner >= 80).astype(jnp.int32)
    factor = jnp.where(mode % MODES == 0, 1.0, 2.0) * (1.0 / (NX * NY * NZ * NT))
    scale[0:384] = factor
    scale[384:768] = factor
    copies = (lax.broadcasted_iota(jnp.int32, (160, CH), 0) // 8 == lanes((160, CH))).astype(F32)
    copies_half = copies.astype(BF)
    same_row = lax.broadcasted_iota(jnp.int32, (160, 160), 0) % 8 == lanes((160, 160)) % 8
    by_out = dot_t(copies_half, point_ref[...]).astype(BF)
    by_in = dot(copies_half, point_ref[...]).astype(BF)
    point_fwd[...] = jnp.where(same_row, dot_t(by_out, copies_half), 0.0).astype(BF)
    point_bwd[...] = jnp.where(same_row, dot_t(by_in, copies_half), 0.0).astype(BF)
    bias_col[...] = jnp.broadcast_to(jnp.sum(copies * bias_ref[...], axis=1, keepdims=True), (160, 128))

    got_yf.wait()
    arrive(sy.at[0], ry.at[0], GY, 0)
    y_forward(ry.at[0], sz.at[0])
    send(sz.at[0], rz.at[0], "gz", g, GZ, 1)
    got_zf.wait()
    got_spread.wait()
    got_gather.wait()
    got_mask.wait()
    arrive(sz.at[0], rz.at[0], GZ, 1)
    spread_u = dot(z_forward(rz.at[0], None), spread[0])
    real_u, imag_u = spread_u[:384], spread_u[384:]
    u0[...] = real_u
    u1[...] = imag_u
    mixed_real = (real_u * w0[...] - imag_u * w1[...]).astype(BF)
    mixed_imag = (real_u * w1[...] + imag_u * w0[...]).astype(BF)
    mixed = jnp.concatenate([mixed_real, mixed_imag], axis=0)
    got_zb.wait()
    z_back(mixed, 1, scale[...], szb.at[0])
    send(szb.at[0], rzb.at[0], "gz", g, GZ, 2)
    got_yb.wait()
    arrive(szb.at[0], rzb.at[0], GZ, 2)
    y_back(rzb.at[0], syb.at[0])
    send(syb.at[0], ryb.at[0], "gy", j, GY, 3)
    got_cot.wait()
    arrive(syb.at[0], ryb.at[0], GY, 3)
    planes_in(ryb.at[0])

    def activate(n, carry):
        cells = pl.ds(pl.multiple_of(n * 256, 256), 256)
        preact = dot(turned[0:160], plane[:, cells]) + dot(point_fwd[...], field[0:160, cells]) + bias_col[:, 0:1]
        normal = 0.5 * (1.0 + lax.erf(preact * 0.7071067811865476))
        density = jnp.exp(-0.5 * preact * preact) * 0.3989422804014327
        layer[:, cells] = (preact * normal).astype(BF)
        slope[0:160, cells] = (cot[:, cells].astype(F32) * (normal + preact * density)).astype(BF)
        return carry

    lax.fori_loop(0, 8, activate, 0)
    planes_out(slope, sy.at[1])
    send(sy.at[1], ry.at[1], "gy", j, GY, 4)
    put_layer = pltpu.make_async_copy(layer, out_hbm, store_sem.at[0])
    put_layer.start()
    arrive(sy.at[1], ry.at[1], GY, 4)
    y_forward(ry.at[1], sz.at[1])
    send(sz.at[1], rz.at[1], "gz", g, GZ, 5)
    arrive(sz.at[1], rz.at[1], GZ, 5)
    spread_g = dot(z_forward(rz.at[1], scale[...]), spread[1])
    real_g, imag_g = spread_g[:384], spread_g[384:]
    mixed_real = (real_g * w0[...] + imag_g * w1[...]).astype(BF)
    mixed_imag = (imag_g * w0[...] - real_g * w1[...]).astype(BF)
    mixed = jnp.concatenate([mixed_real, mixed_imag], axis=0)
    z_back(mixed, 0, None, szb.at[1])
    send(szb.at[1], rzb.at[1], "gz", g, GZ, 6)
    w0[...] = u0[...] * real_g + u1[...] * imag_g
    w1[...] = u0[...] * imag_g - u1[...] * real_g
    arrive(szb.at[1], rzb.at[1], GZ, 6)
    y_back(rzb.at[1], syb.at[1])
    send(syb.at[1], ryb.at[1], "gy", j, GY, 7)
    wg[...] = jnp.zeros((PROWS, 7296), F32)
    for q in range(9):
        for part, held in enumerate((w0, w1)):
            start = 800 * q + 400 * part
            first, shift = start // 128 * 128, start % 128
            top = 128 * (q // 3) + PROWS * (q % 3)
            piece = held[top : top + PROWS]
            if shift:
                piece = pltpu.roll(piece, shift, 1)
            wg[:, first : first + 512] = wg[:, first : first + 512] + piece
    wgrad[...] = wg[0:PAIRS, 0:7200]
    put_wgrad = pltpu.make_async_copy(wgrad, wgrad_hbm, store_sem.at[1])
    put_wgrad.start()
    arrive(syb.at[1], ryb.at[1], GY, 7)
    planes_in(ryb.at[1])

    def finish(n, carry):
        cells = pl.ds(pl.multiple_of(n * 256, 256), 256)
        total = dot(turned[0:160], plane[:, cells]) + dot(point_bwd[...], slope[0:160, cells])
        fgrad[:, cells] = total.astype(BF)
        return carry

    lax.fori_loop(0, 8, finish, 0)
    put_fgrad = pltpu.make_async_copy(fgrad, fgrad_hbm, store_sem.at[2])
    put_fgrad.start()
    put_layer.wait()
    put_wgrad.wait()
    put_fgrad.wait()


def per_device(field, cotangent, spectral_weight, point_weight, channel_bias):
    cells = NX * NT
    flat = field.reshape(160, cells)
    flat_cot = cotangent.reshape(160, cells)
    whole = pl.BlockSpec(memory_space=pltpu.VMEM)
    anywhere = pl.BlockSpec(memory_space=pl.ANY)
    consts = constants()
    vm = pltpu.VMEM
    scratch = [
        vm((256, cells), BF),
        vm((160, cells), BF),
        vm((PAIRS, 7200), BF),
        vm((768, cells), BF),
        vm((1536, 768), BF),
        vm((4032, 384), BF),
        vm((1536, 1024), BF),
        vm((3072, 384), BF),
        vm((2, 256, 512), BF),
        vm((2, 512, 256), BF),
        vm((2, 128, 128), F32),
        vm((256, cells), BF),
        vm((160, cells), BF),
        vm((160, cells), BF),
        vm((PROWS, 7296), F32),
        vm((384, 512), F32),
        vm((384, 512), F32),
        vm((384, 512), F32),
        vm((384, 512), F32),
        vm((PROWS, 7296), F32),
        vm((PAIRS, 7200), F32),
        vm((256, 768), BF),
        vm((768, 128), F32),
        vm((160, 160), BF),
        vm((160, 160), BF),
        vm((160, 128), F32),
        vm((2, GY, SLAB, 128), BF),
        vm((2, GY, SLAB, 128), BF),
        vm((2, GZ, SLAB, 128), BF),
        vm((2, GZ, SLAB, 128), BF),
        vm((2, GZ, SLAB, 128), BF),
        vm((2, GZ, SLAB, 128), BF),
        vm((2, GY, SLAB, 128), BF),
        vm((2, GY, SLAB, 128), BF),
        pltpu.SemaphoreType.DMA((11,)),
        pltpu.SemaphoreType.DMA((3,)),
        pltpu.SemaphoreType.DMA((8,)),
        pltpu.SemaphoreType.DMA((8,)),
    ]
    layer, fgrad, wgrad = pl.pallas_call(
        kernel,
        out_shape=(
            jax.ShapeDtypeStruct((160, cells), BF),
            jax.ShapeDtypeStruct((160, cells), BF),
            jax.ShapeDtypeStruct((PAIRS, 7200), F32),
        ),
        in_specs=[anywhere, anywhere, anywhere, whole, whole] + [anywhere] * len(consts),
        out_specs=(anywhere, anywhere, anywhere),
        scratch_shapes=scratch,
        compiler_params=pltpu.CompilerParams(
            collective_id=0, has_side_effects=True, vmem_limit_bytes=60 * 1024 * 1024
        ),
    )(flat, flat_cot, spectral_weight, point_weight, channel_bias.reshape(1, CH), *consts)
    return layer.reshape(field.shape), fgrad.reshape(field.shape), wgrad


def solution(mesh):
    return jax.shard_map(
        per_device,
        mesh=mesh,
        in_specs=(P(None, "gy", "gz", None), P(None, "gy", "gz", None), P("gz", "gy"), P(), P()),
        out_specs=(P(None, "gy", "gz", None), P(None, "gy", "gz", None), P("gz", "gy")),
        check_vma=False,
    )
```

```python
import functools

import jax
import jax.numpy as jnp
import ml_dtypes
import numpy as np
from jax import lax
from jax.experimental import pallas as pl
from jax.experimental.pallas import tpu as pltpu
from jax.sharding import PartitionSpec as P

MODES = 12
NX = 64
NY = 64
NZ = 64
NT = 32
CH = 20
GY = 32
GZ = 16
PAIRS = 36
PROWS = 40
SLAB = 8
PARTS = 3
LINES = 168
MESH = pl.DeviceIdType.MESH
BF = jnp.bfloat16
F32 = jnp.float32


def kept(slots, length):
    return np.where(slots < MODES, slots, length - 2 * MODES + slots)


def plane_constant():
    cell = np.arange(NX * NT)
    x, t = cell // NT, cell % NT
    out = np.zeros((GY, 3, 8, NX * NT))
    for d in range(GY):
        for k in range(3):
            for q3 in range(3):
                q = 9 * d + 3 * k + q3
                kx, kt = kept(np.array(q // MODES), NX), q % MODES
                angle = 2 * np.pi * ((kx * x % NX) / NX + (kt * t % NT) / NT)
                out[d, k, 2 * q3] = np.cos(angle)
                out[d, k, 2 * q3 + 1] = -np.sin(angle)
    return out.transpose(1, 0, 2, 3).reshape(PARTS, GY * SLAB, NX * NT)


def slot_frequency(length):
    g = np.arange(GZ)[:, None]
    return kept(3 * g // 2 + np.arange(2)[None, :], length)


def on_slabs(cosine, sine):
    rows, cols = cosine.shape
    two = np.stack([np.stack([cosine, sine], -1), np.stack([-sine, cosine], -1)], 2)
    full = np.einsum("rcab,uv->ruacvb", two.transpose(0, 1, 2, 3), np.eye(4))
    return full.reshape(rows * SLAB, cols * SLAB)


def y_constants():
    ky = slot_frequency(NY)
    y = 2 * np.arange(GY)[None, :] + np.arange(2)[:, None]
    angle = 2 * np.pi * (ky[None, :, :, None] * y[:, None, None, :] % NY) / NY
    near = angle.transpose(0, 2, 1, 3)
    forward = on_slabs(np.cos(near).reshape(-1, GY), np.sin(near).reshape(-1, GY))
    far = angle.transpose(0, 2, 3, 1)
    back = on_slabs(np.cos(far).reshape(-1, GZ), -np.sin(far).reshape(-1, GZ))
    return forward, back


def pair_slots(parity):
    p = np.arange(PAIRS) + 12 * parity
    return p // 24, p % 24


def z_constants():
    forward = np.zeros((2, 4, 2, LINES, GZ, 4, 2))
    back = np.zeros((2, 4, GZ, 4, 2, 2, LINES))
    for parity in range(2):
        kz = kept(pair_slots(parity)[1], NZ)
        for zl in range(4):
            angle = 2 * np.pi * (kz[:, None] * (4 * np.arange(GZ) + zl)[None, :] % NZ) / NZ
            c, s = np.cos(angle), np.sin(angle)
            for u in range(4):
                rows = slice(PROWS * u, PROWS * u + PAIRS) if u < 3 else slice(128, 128 + PAIRS)
                forward[parity, zl, 0, rows, :, u, 0] = c
                forward[parity, zl, 0, rows, :, u, 1] = s
                forward[parity, zl, 1, rows, :, u, 0] = -s
                forward[parity, zl, 1, rows, :, u, 1] = c
                back[parity, zl, :, u, 0, 0, rows] = c.T
                back[parity, zl, :, u, 0, 1, rows] = -s.T
                back[parity, zl, :, u, 1, 0, rows] = s.T
                back[parity, zl, :, u, 1, 1, rows] = c.T
    back = np.pad(back.reshape(2, 4 * GZ * SLAB, 2 * LINES), ((0, 0), (0, 0), (0, 384 - 2 * LINES)))
    return forward.reshape(2, 8 * LINES, GZ * SLAB), back


def mask_constant():
    lane = np.arange(128)
    out = np.zeros((2, 2, 128, 128))
    for parity in range(2):
        slot = pair_slots(parity)[0]
        for q3 in range(3):
            rows = slice(PROWS * q3, PROWS * q3 + PAIRS)
            match = (lane // 4 % 2)[None, :] == slot[:, None]
            out[parity, 0, rows] = match
            out[parity, 1, rows] = match & (lane // 32 == q3)[None, :]
    return out


def channel_constants():
    lane = np.arange(128)
    channel = np.concatenate([lane // 8, np.where(lane < 96, 16 + lane % 32 // 8, -1)])
    pair = np.arange(512)
    first = np.where(pair < CH * CH, pair // CH, -2)
    second = np.where(pair < CH * CH, pair % CH, -2)
    return channel[:, None] == first[None, :], channel[:, None] == second[None, :]


@functools.cache
def constants():
    half = lambda a: np.asarray(a, np.float32).astype(ml_dtypes.bfloat16)
    y_forward, y_back = y_constants()
    z_forward, z_back = z_constants()
    first, second = channel_constants()
    spread = np.stack([first, second])
    return (
        half(plane_constant()),
        half(y_forward),
        half(z_forward),
        half(z_back),
        half(y_back),
        half(spread),
        half(spread.transpose(0, 2, 1)),
        np.asarray(mask_constant(), np.float32),
    )


def dot(a, b):
    return jnp.dot(a, b, preferred_element_type=F32)


def dot_t(a, b):
    return lax.dot_general(a, b, (((1,), (1,)), ((), ())), preferred_element_type=F32)


def lanes(shape):
    return lax.broadcasted_iota(jnp.int32, shape, len(shape) - 1)


def kernel(
    field_hbm, cot_hbm, weight_hbm, point_ref, bias_ref,
    plane_hbm, yf_hbm, zf_hbm, zb_hbm, yb_hbm, spread_hbm, gather_hbm, mask_hbm,
    out_hbm, fgrad_hbm, wgrad_hbm,
    field, cot, weight, plane, yf, zf, zb, yb, spread, gather, mask,
    slope, layer, fgrad, wf, w0, w1, u0, u1, wg, wgrad, volume, turned, scale, point_fwd, point_bwd, bias_col,
    sy, ry, sz, rz, szb, rzb, syb, ryb, load_sem, store_sem, send_sem, recv_sem,
):
    j = lax.axis_index("gy")
    g = lax.axis_index("gz")
    parity = lax.rem(g, 2)

    def load(i, src, dst):
        copy = pltpu.make_async_copy(src, dst, load_sem.at[i])
        copy.start()
        return copy

    got_field = load(0, field_hbm, field.at[pl.ds(0, 160)])
    got_plane = [load(1 + k, plane_hbm.at[k], plane.at[k]) for k in range(PARTS)]
    got_yf = load(4, yf_hbm, yf)
    got_weight = load(5, weight_hbm, weight)
    got_zf = load(6, zf_hbm.at[parity], zf)
    got_spread = load(7, spread_hbm, spread)
    got_gather = load(8, gather_hbm, gather)
    got_mask = load(9, mask_hbm.at[parity], mask)
    got_zb = load(10, zb_hbm.at[parity], zb)
    got_yb = load(11, yb_hbm, yb)
    got_cot = load(12, cot_hbm, cot)

    barrier = pltpu.get_barrier_semaphore()

    def greet(axis, me, count):
        def one(k, carry):
            pl.semaphore_signal(barrier, inc=1, device_id={axis: lax.rem(me + k, count)}, device_id_type=MESH)
            return carry

        lax.fori_loop(1, count, one, 0)

    greet("gy", j, GY)
    greet("gz", g, GZ)

    def copy_to(src, dst, axis, me, other, which):
        pltpu.make_async_remote_copy(
            src_ref=src.at[other],
            dst_ref=dst.at[me],
            send_sem=send_sem.at[which],
            recv_sem=recv_sem.at[which],
            device_id={axis: other},
            device_id_type=MESH,
        ).start()

    def send_y(src, dst, which):
        near = j // 16 * 16
        far = 16 - near
        z = lax.rem(j, 16)
        half = lax.rem(z + 8, 16)
        copy_to(src, dst, "gy", j, near + half, which)
        copy_to(src, dst, "gy", j, far + half, which)

        def one(i, carry):
            up = lax.rem(z + 8 - i, 16)
            down = lax.rem(z + 8 + i, 16)
            copy_to(src, dst, "gy", j, far + up, which)
            copy_to(src, dst, "gy", j, far + down, which)
            copy_to(src, dst, "gy", j, near + up, which)
            copy_to(src, dst, "gy", j, near + down, which)
            return carry

        lax.fori_loop(1, 8, one, 0)
        copy_to(src, dst, "gy", j, far + z, which)
        dst[pl.ds(j, 1)] = src[pl.ds(j, 1)]

    def send_z(src, dst, which):
        def one(i, carry):
            copy_to(src, dst, "gz", g, lax.rem(g + 8 + i, 16), which)
            copy_to(src, dst, "gz", g, lax.rem(g + 8 - i, 16), which)
            return carry

        copy_to(src, dst, "gz", g, lax.rem(g + 8, 16), which)
        lax.fori_loop(1, 8, one, 0)
        dst[pl.ds(g, 1)] = src[pl.ds(g, 1)]

    def arrive(dst, count, which):
        part = pl.ds(0, count - 1)
        pltpu.make_async_copy(dst.at[part], dst.at[part], recv_sem.at[which]).wait()

    def sent(src, count, which):
        part = pl.ds(0, count - 1)
        pltpu.make_async_copy(src.at[part], src.at[part], send_sem.at[which]).wait()

    zlane = lanes((1, 128)) % 4
    low_slot = lanes((1, 128)) // 4 % 2 == 0
    row3 = lax.broadcasted_iota(jnp.int32, (1, 8, 128), 1)
    lane3 = lanes((1, 8, 128))

    def planes_out(source, k, buffer):
        full = dot_t(plane[k], source[...])
        main = full[:, :128].reshape(GY, 8, 128)
        left = full[:, 128:].reshape(GY, 8, 128)
        extra = jnp.zeros_like(main)
        for q3 in range(3):
            moved = pltpu.roll(left, 6 - 2 * q3, 1)
            if q3:
                moved = pltpu.roll(moved, 32 * q3, 2)
            extra = jnp.where(lane3 // 32 == q3, moved, extra)
        buffer[...] = jnp.where(row3 >= 6, extra, main).astype(BF)

    def planes_in(buffer, k):
        block = buffer[...].astype(F32)
        left = jnp.zeros_like(block)
        for q3 in range(3):
            moved = pltpu.roll(block, 2 + 2 * q3, 1)
            if q3:
                moved = pltpu.roll(moved, 128 - 32 * q3, 2)
            left = jnp.where(row3 // 2 == q3, moved, left)
        turned[k, 0:128] = block.reshape(256, 128).T.astype(BF)
        turned[k, 128:256] = left.reshape(256, 128).T.astype(BF)

    def swap_slots(same_low, same_high, cross_low, cross_high):
        crossed = jnp.where(low_slot, pltpu.roll(cross_low, 124, 1), pltpu.roll(cross_high, 4, 1))
        return jnp.where(low_slot, same_low, same_high) + crossed

    def y_forward(buffer, target):
        block = buffer[...].reshape(256, 128)
        part = [dot(yf[128 * n : 128 * n + 128], block) for n in range(4)]
        target[...] = swap_slots(part[0], part[3], part[2], part[1]).reshape(GZ, SLAB, 128).astype(BF)

    def y_back(buffer, target):
        block = buffer[...].reshape(128, 128)
        part = [dot(yb[256 * n : 256 * n + 256], block) for n in range(4)]
        target[...] = swap_slots(part[0], part[3], part[1], part[2]).reshape(GY, SLAB, 128).astype(BF)

    def by_z(parts):
        low = jnp.where(zlane == 0, parts[0], parts[1])
        high = jnp.where(zlane == 2, parts[2], parts[3])
        return jnp.where(zlane < 2, low, high)

    def z_forward(buffer, factor):
        block = buffer[...].reshape(128, 128)
        step = 2 * LINES
        values = by_z([dot(zf[step * n : step * n + step], block) for n in range(4)]).reshape(2, LINES, 128)
        left = values[:, 128:]
        left = jnp.concatenate([left, left, left, jnp.zeros((2, 8, 128), F32)], axis=1)
        main = values[:, :128] * mask[0:1]
        left = left * mask[1:2]
        if factor is not None:
            main, left = main * factor[None], left * factor[None]
        return jnp.concatenate([main.reshape(256, 128).astype(BF), left.reshape(256, 128).astype(BF)], axis=1)

    def z_back(mixed, n, factor, target):
        values = dot(mixed, gather[n])
        main = values[:, :128].reshape(2, 128, 128) * mask[0:1]
        left = values[:, 128:].reshape(2, 128, 128) * mask[1:2]
        if factor is not None:
            main, left = main * factor[None], left * factor[None]
        left = left[:, 0:40] + left[:, 40:80] + left[:, 80:120]
        rows = jnp.concatenate([main, left], axis=1).reshape(2 * LINES, 128)
        rows = jnp.concatenate([rows, jnp.zeros((384 - 2 * LINES, 128), F32)], axis=0).astype(BF)
        parts = [dot(zb[128 * n : 128 * n + 128], rows) for n in range(4)]
        target[...] = by_z(parts).reshape(GZ, SLAB, 128).astype(BF)

    def mix_forward(k):
        spread_u = dot(z_forward(rz.at[0, k], None), spread[0])
        real_u, imag_u = spread_u[:128], spread_u[128:]
        u0[k] = real_u
        u1[k] = imag_u
        mixed_real = (real_u * w0[k] - imag_u * w1[k]).astype(BF)
        mixed_imag = (real_u * w1[k] + imag_u * w0[k]).astype(BF)
        z_back(jnp.concatenate([mixed_real, mixed_imag], axis=0), 1, scale[k], szb.at[0, k])

    def mix_back(k):
        spread_g = dot(z_forward(rz.at[1, k], scale[k]), spread[1])
        real_g, imag_g = spread_g[:128], spread_g[128:]
        mixed_real = (real_g * w0[k] + imag_g * w1[k]).astype(BF)
        mixed_imag = (imag_g * w0[k] - real_g * w1[k]).astype(BF)
        z_back(jnp.concatenate([mixed_real, mixed_imag], axis=0), 0, None, szb.at[1, k])
        w0[k] = u0[k] * real_g + u1[k] * imag_g
        w1[k] = u0[k] * imag_g - u1[k] * real_g

    def align_weights():
        wf[...] = jnp.zeros((PROWS, 7296), F32)
        wf[0:PAIRS, 0:7200] = weight[...].astype(F32)
        w0[...] = jnp.zeros((PARTS, 128, 512), F32)
        w1[...] = jnp.zeros((PARTS, 128, 512), F32)
        for q in range(9):
            for part, held in enumerate((w0, w1)):
                start = 800 * q + 400 * part
                first, shift = start // 128 * 128, start % 128
                piece = wf[:, first : first + 512]
                if shift:
                    piece = pltpu.roll(piece, 512 - shift, 1)
                top = PROWS * (q % 3)
                held[q // 3, top : top + PROWS] = piece

    def return_weights():
        wg[...] = jnp.zeros((PROWS, 7296), F32)
        for q in range(9):
            for part, held in enumerate((w0, w1)):
                start = 800 * q + 400 * part
                first, shift = start // 128 * 128, start % 128
                top = PROWS * (q % 3)
                piece = held[q // 3, top : top + PROWS]
                if shift:
                    piece = pltpu.roll(piece, shift, 1)
                wg[:, first : first + 512] = wg[:, first : first + 512] + piece
        wgrad[...] = wg[0:PAIRS, 0:7200]

    def small_tables():
        row = lax.broadcasted_iota(jnp.int32, (128, 128), 0)
        for k in range(PARTS):
            mode = 9 * j + 3 * k + (row >= 40).astype(jnp.int32) + (row >= 80).astype(jnp.int32)
            scale[k] = jnp.where(mode % MODES == 0, 1.0, 2.0) * (1.0 / (NX * NY * NZ * NT))
        copies = (lax.broadcasted_iota(jnp.int32, (160, CH), 0) // 8 == lanes((160, CH))).astype(F32)
        copies_half = copies.astype(BF)
        same_row = lax.broadcasted_iota(jnp.int32, (160, 160), 0) % 8 == lanes((160, 160)) % 8
        by_out = dot_t(copies_half, point_ref[...]).astype(BF)
        by_in = dot(copies_half, point_ref[...]).astype(BF)
        point_fwd[...] = jnp.where(same_row, dot_t(by_out, copies_half), 0.0).astype(BF)
        point_bwd[...] = jnp.where(same_row, dot_t(by_in, copies_half), 0.0).astype(BF)
        bias_col[...] = jnp.broadcast_to(jnp.sum(copies * bias_ref[...], axis=1, keepdims=True), (160, 128))

    def each_chunk(step):
        def one(n, carry):
            step(pl.ds(pl.multiple_of(n * 256, 256), 256))
            return carry

        lax.fori_loop(0, NX * NT // 256, one, 0)

    def point_forward(cells):
        volume[:, cells] = dot(point_fwd[...], field[0:160, cells]) + bias_col[:, 0:1]

    def point_back(cells):
        volume[:, cells] = dot(point_bwd[...], slope[0:160, cells])

    def summed(k, cells):
        return volume[:, cells] + dot(turned[k, 0:160], plane[k, :, cells])

    def add_part(k):
        def step(cells):
            volume[:, cells] = summed(k, cells)

        planes_in(ryb.at[now[0], k], k)
        each_chunk(step)

    def activate(cells):
        preact = summed(2, cells)
        normal = 0.5 * (1.0 + lax.erf(preact * 0.7071067811865476))
        density = jnp.exp(-0.5 * preact * preact) * 0.3989422804014327
        layer[:, cells] = (preact * normal).astype(BF)
        slope[0:160, cells] = (cot[:, cells].astype(F32) * (normal + preact * density)).astype(BF)

    def finish(cells):
        fgrad[:, cells] = summed(2, cells).astype(BF)

    now = [0]

    def start_part(source, k):
        t = now[0]
        planes_out(source, k, sy.at[t, k])
        if t == 0 and k == 0:
            pl.semaphore_wait(barrier, GY + GZ - 2)
        send_y(sy.at[t, k], ry.at[t, k], 12 * t + k)

    def y_part(k):
        t = now[0]
        arrive(ry.at[t, k], GY, 12 * t + k)
        y_forward(ry.at[t, k], sz.at[t, k])
        send_z(sz.at[t, k], rz.at[t, k], 12 * t + 3 + k)

    def z_part(k):
        t = now[0]
        arrive(rz.at[t, k], GZ, 12 * t + 3 + k)
        if t == 0:
            mix_forward(k)
        else:
            mix_back(k)
        send_z(szb.at[t, k], rzb.at[t, k], 12 * t + 6 + k)

    def back_part(k):
        t = now[0]
        arrive(rzb.at[t, k], GZ, 12 * t + 6 + k)
        y_back(rzb.at[t, k], syb.at[t, k])
        send_y(syb.at[t, k], ryb.at[t, k], 12 * t + 9 + k)

    def end_part(k):
        arrive(ryb.at[now[0], k], GY, 12 * now[0] + 9 + k)

    field[160:256] = jnp.zeros((96, NX * NT), BF)
    slope[160:256] = jnp.zeros((96, NX * NT), BF)
    got_field.wait()
    for k in range(PARTS):
        got_plane[k].wait()
        start_part(field, k)
    got_weight.wait()
    align_weights()
    small_tables()
    each_chunk(point_forward)
    got_yf.wait()
    y_part(0)
    got_zf.wait()
    got_spread.wait()
    got_gather.wait()
    got_mask.wait()
    got_zb.wait()
    got_yb.wait()
    got_cot.wait()
    y_part(1)
    z_part(0)
    y_part(2)
    z_part(1)
    back_part(0)
    z_part(2)
    back_part(1)
    back_part(2)
    for k in range(2):
        end_part(k)
        add_part(k)
    end_part(2)
    planes_in(ryb.at[0, 2], 2)
    each_chunk(activate)
    put_layer = pltpu.make_async_copy(layer, out_hbm, store_sem.at[0])
    now[0] = 1
    for k in range(PARTS):
        start_part(slope, k)
    put_layer.start()
    each_chunk(point_back)
    y_part(0)
    y_part(1)
    z_part(0)
    y_part(2)
    z_part(1)
    back_part(0)
    z_part(2)
    back_part(1)
    back_part(2)
    return_weights()
    put_wgrad = pltpu.make_async_copy(wgrad, wgrad_hbm, store_sem.at[1])
    put_wgrad.start()
    for k in range(2):
        end_part(k)
        add_part(k)
    end_part(2)
    planes_in(ryb.at[1, 2], 2)
    each_chunk(finish)
    put_fgrad = pltpu.make_async_copy(fgrad, fgrad_hbm, store_sem.at[2])
    put_fgrad.start()
    for t in range(2):
        for k in range(PARTS):
            sent(sy.at[t, k], GY, 12 * t + k)
            sent(sz.at[t, k], GZ, 12 * t + 3 + k)
            sent(szb.at[t, k], GZ, 12 * t + 6 + k)
            sent(syb.at[t, k], GY, 12 * t + 9 + k)
    put_layer.wait()
    put_wgrad.wait()
    put_fgrad.wait()


def per_device(field, cotangent, spectral_weight, point_weight, channel_bias):
    cells = NX * NT
    flat = field.reshape(160, cells)
    flat_cot = cotangent.reshape(160, cells)
    whole = pl.BlockSpec(memory_space=pltpu.VMEM)
    anywhere = pl.BlockSpec(memory_space=pl.ANY)
    consts = constants()
    vm = pltpu.VMEM
    scratch = [
        vm((256, cells), BF),
        vm((160, cells), BF),
        vm((PAIRS, 7200), BF),
        vm((PARTS, 256, cells), BF),
        vm((512, 256), BF),
        vm((8 * LINES, 128), BF),
        vm((512, 384), BF),
        vm((1024, 128), BF),
        vm((2, 256, 512), BF),
        vm((2, 512, 256), BF),
        vm((2, 128, 128), F32),
        vm((256, cells), BF),
        vm((160, cells), BF),
        vm((160, cells), BF),
        vm((PROWS, 7296), F32),
        vm((PARTS, 128, 512), F32),
        vm((PARTS, 128, 512), F32),
        vm((PARTS, 128, 512), F32),
        vm((PARTS, 128, 512), F32),
        vm((PROWS, 7296), F32),
        vm((PAIRS, 7200), F32),
        vm((160, cells), F32),
        vm((PARTS, 256, 256), BF),
        vm((PARTS, 128, 128), F32),
        vm((160, 160), BF),
        vm((160, 160), BF),
        vm((160, 128), F32),
        vm((2, PARTS, GY, SLAB, 128), BF),
        vm((2, PARTS, GY, SLAB, 128), BF),
        vm((2, PARTS, GZ, SLAB, 128), BF),
        vm((2, PARTS, GZ, SLAB, 128), BF),
        vm((2, PARTS, GZ, SLAB, 128), BF),
        vm((2, PARTS, GZ, SLAB, 128), BF),
        vm((2, PARTS, GY, SLAB, 128), BF),
        vm((2, PARTS, GY, SLAB, 128), BF),
        pltpu.SemaphoreType.DMA((13,)),
        pltpu.SemaphoreType.DMA((3,)),
        pltpu.SemaphoreType.DMA((24,)),
        pltpu.SemaphoreType.DMA((24,)),
    ]
    layer, fgrad, wgrad = pl.pallas_call(
        kernel,
        out_shape=(
            jax.ShapeDtypeStruct((160, cells), BF),
            jax.ShapeDtypeStruct((160, cells), BF),
            jax.ShapeDtypeStruct((PAIRS, 7200), F32),
        ),
        in_specs=[anywhere, anywhere, anywhere, whole, whole] + [anywhere] * len(consts),
        out_specs=(anywhere, anywhere, anywhere),
        scratch_shapes=scratch,
        compiler_params=pltpu.CompilerParams(
            collective_id=0, has_side_effects=True, vmem_limit_bytes=60 * 1024 * 1024
        ),
    )(flat, flat_cot, spectral_weight, point_weight, channel_bias.reshape(1, CH), *consts)
    return layer.reshape(field.shape), fgrad.reshape(field.shape), wgrad


def solution(mesh):
    return jax.shard_map(
        per_device,
        mesh=mesh,
        in_specs=(P(None, "gy", "gz", None), P(None, "gy", "gz", None), P("gz", "gy"), P(), P()),
        out_specs=(P(None, "gy", "gz", None), P(None, "gy", "gz", None), P("gz", "gy")),
        check_vma=False,
    )
```

```python
import functools

import jax
import jax.numpy as jnp
import ml_dtypes
import numpy as np
from jax import lax
from jax.experimental import pallas as pl
from jax.experimental.pallas import tpu as pltpu
from jax.sharding import PartitionSpec as P

MODES = 12
NX = 64
NY = 64
NZ = 64
NT = 32
CH = 20
GY = 32
GZ = 16
PAIRS = 36
PROWS = 40
SLAB = 8
PARTS = 3
LINES = 168
MESH = pl.DeviceIdType.MESH
BF = jnp.bfloat16
F32 = jnp.float32


def kept(slots, length):
    return np.where(slots < MODES, slots, length - 2 * MODES + slots)


def plane_constant():
    cell = np.arange(NX * NT)
    x, t = cell // NT, cell % NT
    out = np.zeros((GY, 3, 8, NX * NT))
    for d in range(GY):
        for k in range(3):
            for q3 in range(3):
                q = 9 * d + 3 * k + q3
                kx, kt = kept(np.array(q // MODES), NX), q % MODES
                angle = 2 * np.pi * ((kx * x % NX) / NX + (kt * t % NT) / NT)
                out[d, k, 2 * q3] = np.cos(angle)
                out[d, k, 2 * q3 + 1] = -np.sin(angle)
    return out.transpose(1, 0, 2, 3).reshape(PARTS, GY * SLAB, NX * NT)


def slot_frequency(length):
    g = np.arange(GZ)[:, None]
    return kept(3 * g // 2 + np.arange(2)[None, :], length)


def on_slabs(cosine, sine):
    rows, cols = cosine.shape
    two = np.stack([np.stack([cosine, sine], -1), np.stack([-sine, cosine], -1)], 2)
    full = np.einsum("rcab,uv->ruacvb", two.transpose(0, 1, 2, 3), np.eye(4))
    return full.reshape(rows * SLAB, cols * SLAB)


def y_constants():
    ky = slot_frequency(NY)
    y = 2 * np.arange(GY)[None, :] + np.arange(2)[:, None]
    angle = 2 * np.pi * (ky[None, :, :, None] * y[:, None, None, :] % NY) / NY
    near = angle.transpose(0, 2, 1, 3)
    forward = on_slabs(np.cos(near).reshape(-1, GY), np.sin(near).reshape(-1, GY))
    far = angle.transpose(0, 2, 3, 1)
    back = on_slabs(np.cos(far).reshape(-1, GZ), -np.sin(far).reshape(-1, GZ))
    return forward, back


def pair_slots(parity):
    p = np.arange(PAIRS) + 12 * parity
    return p // 24, p % 24


def z_constants():
    forward = np.zeros((2, 4, 2, LINES, GZ, 4, 2))
    back = np.zeros((2, 4, GZ, 4, 2, 2, LINES))
    for parity in range(2):
        kz = kept(pair_slots(parity)[1], NZ)
        for zl in range(4):
            angle = 2 * np.pi * (kz[:, None] * (4 * np.arange(GZ) + zl)[None, :] % NZ) / NZ
            c, s = np.cos(angle), np.sin(angle)
            for u in range(4):
                rows = slice(PROWS * u, PROWS * u + PAIRS) if u < 3 else slice(128, 128 + PAIRS)
                forward[parity, zl, 0, rows, :, u, 0] = c
                forward[parity, zl, 0, rows, :, u, 1] = s
                forward[parity, zl, 1, rows, :, u, 0] = -s
                forward[parity, zl, 1, rows, :, u, 1] = c
                back[parity, zl, :, u, 0, 0, rows] = c.T
                back[parity, zl, :, u, 0, 1, rows] = -s.T
                back[parity, zl, :, u, 1, 0, rows] = s.T
                back[parity, zl, :, u, 1, 1, rows] = c.T
    back = np.pad(back.reshape(2, 4 * GZ * SLAB, 2 * LINES), ((0, 0), (0, 0), (0, 384 - 2 * LINES)))
    return forward.reshape(2, 8 * LINES, GZ * SLAB), back


def mask_constant():
    lane = np.arange(128)
    out = np.zeros((2, 2, 128, 128))
    for parity in range(2):
        slot = pair_slots(parity)[0]
        for q3 in range(3):
            rows = slice(PROWS * q3, PROWS * q3 + PAIRS)
            match = (lane // 4 % 2)[None, :] == slot[:, None]
            out[parity, 0, rows] = match
            out[parity, 1, rows] = match & (lane // 32 == q3)[None, :]
    return out


def channel_constants():
    lane = np.arange(128)
    channel = np.concatenate([lane // 8, np.where(lane < 96, 16 + lane % 32 // 8, -1)])
    pair = np.arange(512)
    first = np.where(pair < CH * CH, pair // CH, -2)
    second = np.where(pair < CH * CH, pair % CH, -2)
    return channel[:, None] == first[None, :], channel[:, None] == second[None, :]


@functools.cache
def constants():
    half = lambda a: np.asarray(a, np.float32).astype(ml_dtypes.bfloat16)
    y_forward, y_back = y_constants()
    z_forward, z_back = z_constants()
    first, second = channel_constants()
    spread = np.stack([first, second])
    return (
        half(plane_constant()),
        half(y_forward),
        half(z_forward),
        half(z_back),
        half(y_back),
        half(spread),
        half(spread.transpose(0, 2, 1)),
        np.asarray(mask_constant(), np.float32),
    )


def dot(a, b):
    return jnp.dot(a, b, preferred_element_type=F32)


def dot_t(a, b):
    return lax.dot_general(a, b, (((1,), (1,)), ((), ())), preferred_element_type=F32)


def lanes(shape):
    return lax.broadcasted_iota(jnp.int32, shape, len(shape) - 1)


def kernel(
    field_hbm, cot_hbm, weight_hbm, point_ref, bias_ref,
    plane_hbm, yf_hbm, zf_hbm, zb_hbm, yb_hbm, spread_hbm, gather_hbm, mask_hbm,
    out_hbm, fgrad_hbm, wgrad_hbm,
    field, cot, weight, plane, yf, zf, zb, yb, spread, gather, mask,
    slope, layer, wf, w0, w1, u0, u1, wg, wgrad, volume, turned, scale, point_fwd, point_bwd, bias_col,
    field_raw, cot_raw, layer_raw, fgrad_raw,
    sy, ry, sz, rz, szb, rzb, syb, ryb, load_sem, store_sem, send_sem, recv_sem,
):
    j = lax.axis_index("gy")
    g = lax.axis_index("gz")
    parity = lax.rem(g, 2)

    barrier = pltpu.get_barrier_semaphore()

    def greet(axis, other):
        pl.semaphore_signal(barrier, inc=1, device_id={axis: other}, device_id_type=MESH)

    def greet_y():
        near = j // 16 * 16
        far = 16 - near
        z = lax.rem(j, 16)
        half = lax.rem(z + 8, 16)
        greet("gy", far + half)
        greet("gy", near + half)

        def one(i, carry):
            up = lax.rem(z + 8 - i, 16)
            down = lax.rem(z + 8 + i, 16)
            greet("gy", far + up)
            greet("gy", far + down)
            greet("gy", near + up)
            greet("gy", near + down)
            return carry

        lax.fori_loop(1, 8, one, 0)
        greet("gy", far + z)

    def greet_z():
        def one(i, carry):
            greet("gz", lax.rem(g + i, 16))
            return carry

        lax.fori_loop(1, 16, one, 0)

    greet_y()
    greet_z()

    def load(i, src, dst):
        copy = pltpu.make_async_copy(src, dst, load_sem.at[i])
        copy.start()
        return copy

    got_field = load(0, field_hbm, field_raw)
    got_plane = [load(1 + k, plane_hbm.at[k], plane.at[k]) for k in range(PARTS)]
    got_yf = load(4, yf_hbm, yf)
    got_weight = load(5, weight_hbm, weight)
    got_zf = load(6, zf_hbm.at[parity], zf)
    got_spread = load(7, spread_hbm, spread)
    got_gather = load(8, gather_hbm, gather)
    got_mask = load(9, mask_hbm.at[parity], mask)
    got_zb = load(10, zb_hbm.at[parity], zb)
    got_yb = load(11, yb_hbm, yb)
    got_cot = load(12, cot_hbm, cot_raw)

    def copy_to(src, dst, axis, me, other, which):
        pltpu.make_async_remote_copy(
            src_ref=src.at[other],
            dst_ref=dst.at[me],
            send_sem=send_sem.at[which],
            recv_sem=recv_sem.at[which],
            device_id={axis: other},
            device_id_type=MESH,
        ).start()

    def send_y(src, dst, which):
        near = j // 16 * 16
        far = 16 - near
        z = lax.rem(j, 16)
        half = lax.rem(z + 8, 16)
        copy_to(src, dst, "gy", j, near + half, which)
        copy_to(src, dst, "gy", j, far + half, which)

        def one(i, carry):
            up = lax.rem(z + 8 - i, 16)
            down = lax.rem(z + 8 + i, 16)
            copy_to(src, dst, "gy", j, far + up, which)
            copy_to(src, dst, "gy", j, far + down, which)
            copy_to(src, dst, "gy", j, near + up, which)
            copy_to(src, dst, "gy", j, near + down, which)
            return carry

        lax.fori_loop(1, 8, one, 0)
        copy_to(src, dst, "gy", j, far + z, which)
        dst[pl.ds(j, 1)] = src[pl.ds(j, 1)]

    def send_z(src, dst, which):
        def one(i, carry):
            copy_to(src, dst, "gz", g, lax.rem(g + 8 + i, 16), which)
            copy_to(src, dst, "gz", g, lax.rem(g + 8 - i, 16), which)
            return carry

        copy_to(src, dst, "gz", g, lax.rem(g + 8, 16), which)
        lax.fori_loop(1, 8, one, 0)
        dst[pl.ds(g, 1)] = src[pl.ds(g, 1)]

    def arrive(dst, count, which):
        part = pl.ds(0, count - 1)
        pltpu.make_async_copy(dst.at[part], dst.at[part], recv_sem.at[which]).wait()

    def sent(src, count, which):
        part = pl.ds(0, count - 1)
        pltpu.make_async_copy(src.at[part], src.at[part], send_sem.at[which]).wait()

    zlane = lanes((1, 128)) % 4
    low_slot = lanes((1, 128)) // 4 % 2 == 0
    row3 = lax.broadcasted_iota(jnp.int32, (1, 8, 128), 1)
    lane3 = lanes((1, 8, 128))

    def planes_out(source, k, buffer):
        full = dot_t(plane[k], source[...])
        main = full[:, :128].reshape(GY, 8, 128)
        left = full[:, 128:].reshape(GY, 8, 128)
        extra = jnp.zeros_like(main)
        for q3 in range(3):
            moved = pltpu.roll(left, 6 - 2 * q3, 1)
            if q3:
                moved = pltpu.roll(moved, 32 * q3, 2)
            extra = jnp.where(lane3 // 32 == q3, moved, extra)
        buffer[...] = jnp.where(row3 >= 6, extra, main).astype(BF)

    def planes_in(buffer, k):
        block = buffer[...].astype(F32)
        left = jnp.zeros_like(block)
        for q3 in range(3):
            moved = pltpu.roll(block, 2 + 2 * q3, 1)
            if q3:
                moved = pltpu.roll(moved, 128 - 32 * q3, 2)
            left = jnp.where(row3 // 2 == q3, moved, left)
        turned[k, 0:128] = block.reshape(256, 128).T.astype(BF)
        turned[k, 128:256] = left.reshape(256, 128).T.astype(BF)

    def swap_slots(same_low, same_high, cross_low, cross_high):
        crossed = jnp.where(low_slot, pltpu.roll(cross_low, 124, 1), pltpu.roll(cross_high, 4, 1))
        return jnp.where(low_slot, same_low, same_high) + crossed

    def y_forward(buffer, target):
        block = buffer[...].reshape(256, 128)
        part = [dot(yf[128 * n : 128 * n + 128], block) for n in range(4)]
        target[...] = swap_slots(part[0], part[3], part[2], part[1]).reshape(GZ, SLAB, 128).astype(BF)

    def y_back(buffer, target):
        block = buffer[...].reshape(128, 128)
        part = [dot(yb[256 * n : 256 * n + 256], block) for n in range(4)]
        target[...] = swap_slots(part[0], part[3], part[1], part[2]).reshape(GY, SLAB, 128).astype(BF)

    def by_z(parts):
        low = jnp.where(zlane == 0, parts[0], parts[1])
        high = jnp.where(zlane == 2, parts[2], parts[3])
        return jnp.where(zlane < 2, low, high)

    def z_forward(buffer, factor):
        block = buffer[...].reshape(128, 128)
        step = 2 * LINES
        values = by_z([dot(zf[step * n : step * n + step], block) for n in range(4)]).reshape(2, LINES, 128)
        left = values[:, 128:]
        left = jnp.concatenate([left, left, left, jnp.zeros((2, 8, 128), F32)], axis=1)
        main = values[:, :128] * mask[0:1]
        left = left * mask[1:2]
        if factor is not None:
            main, left = main * factor[None], left * factor[None]
        return jnp.concatenate([main.reshape(256, 128).astype(BF), left.reshape(256, 128).astype(BF)], axis=1)

    def z_back(mixed, n, factor, target):
        values = dot(mixed, gather[n])
        main = values[:, :128].reshape(2, 128, 128) * mask[0:1]
        left = values[:, 128:].reshape(2, 128, 128) * mask[1:2]
        if factor is not None:
            main, left = main * factor[None], left * factor[None]
        left = left[:, 0:40] + left[:, 40:80] + left[:, 80:120]
        rows = jnp.concatenate([main, left], axis=1).reshape(2 * LINES, 128)
        rows = jnp.concatenate([rows, jnp.zeros((384 - 2 * LINES, 128), F32)], axis=0).astype(BF)
        parts = [dot(zb[128 * n : 128 * n + 128], rows) for n in range(4)]
        target[...] = by_z(parts).reshape(GZ, SLAB, 128).astype(BF)

    def mix_forward(k):
        spread_u = dot(z_forward(rz.at[0, k], None), spread[0])
        real_u, imag_u = spread_u[:128], spread_u[128:]
        u0[k] = real_u
        u1[k] = imag_u
        mixed_real = (real_u * w0[k] - imag_u * w1[k]).astype(BF)
        mixed_imag = (real_u * w1[k] + imag_u * w0[k]).astype(BF)
        z_back(jnp.concatenate([mixed_real, mixed_imag], axis=0), 1, scale[k], szb.at[0, k])

    def mix_back(k):
        spread_g = dot(z_forward(rz.at[1, k], scale[k]), spread[1])
        real_g, imag_g = spread_g[:128], spread_g[128:]
        mixed_real = (real_g * w0[k] + imag_g * w1[k]).astype(BF)
        mixed_imag = (imag_g * w0[k] - real_g * w1[k]).astype(BF)
        z_back(jnp.concatenate([mixed_real, mixed_imag], axis=0), 0, None, szb.at[1, k])
        w0[k] = u0[k] * real_g + u1[k] * imag_g
        w1[k] = u0[k] * imag_g - u1[k] * real_g

    def align_weights():
        wf[...] = jnp.zeros((PROWS, 7296), F32)
        wf[0:PAIRS, 0:7200] = weight[...].astype(F32)
        w0[...] = jnp.zeros((PARTS, 128, 512), F32)
        w1[...] = jnp.zeros((PARTS, 128, 512), F32)
        for q in range(9):
            for part, held in enumerate((w0, w1)):
                start = 800 * q + 400 * part
                first, shift = start // 128 * 128, start % 128
                piece = wf[:, first : first + 512]
                if shift:
                    piece = pltpu.roll(piece, 512 - shift, 1)
                top = PROWS * (q % 3)
                held[q // 3, top : top + PROWS] = piece

    def return_weights():
        wg[...] = jnp.zeros((PROWS, 7296), F32)
        for q in range(9):
            for part, held in enumerate((w0, w1)):
                start = 800 * q + 400 * part
                first, shift = start // 128 * 128, start % 128
                top = PROWS * (q % 3)
                piece = held[q // 3, top : top + PROWS]
                if shift:
                    piece = pltpu.roll(piece, shift, 1)
                wg[:, first : first + 512] = wg[:, first : first + 512] + piece
        wgrad[...] = wg[0:PAIRS, 0:7200]

    def small_tables():
        row = lax.broadcasted_iota(jnp.int32, (128, 128), 0)
        for k in range(PARTS):
            mode = 9 * j + 3 * k + (row >= 40).astype(jnp.int32) + (row >= 80).astype(jnp.int32)
            scale[k] = jnp.where(mode % MODES == 0, 1.0, 2.0) * (1.0 / (NX * NY * NZ * NT))
        copies = (lax.broadcasted_iota(jnp.int32, (160, CH), 0) // 8 == lanes((160, CH))).astype(F32)
        copies_half = copies.astype(BF)
        same_row = lax.broadcasted_iota(jnp.int32, (160, 160), 0) % 8 == lanes((160, 160)) % 8
        by_out = dot_t(copies_half, point_ref[...]).astype(BF)
        by_in = dot(copies_half, point_ref[...]).astype(BF)
        point_fwd[...] = jnp.where(same_row, dot_t(by_out, copies_half), 0.0).astype(BF)
        point_bwd[...] = jnp.where(same_row, dot_t(by_in, copies_half), 0.0).astype(BF)
        bias_col[...] = jnp.broadcast_to(jnp.sum(copies * bias_ref[...], axis=1, keepdims=True), (160, 128))

    def each_chunk(step):
        def one(n, carry):
            step(pl.ds(pl.multiple_of(n * 256, 256), 256))
            return carry

        lax.fori_loop(0, NX * NT // 256, one, 0)

    def point_forward(cells):
        volume[:, cells] = dot(point_fwd[...], field[0:160, cells]) + bias_col[:, 0:1]

    def point_back(cells):
        volume[:, cells] = dot(point_bwd[...], slope[0:160, cells])

    def summed(k, cells):
        return volume[:, cells] + dot(turned[k, 0:160], plane[k, :, cells])

    def add_part(k):
        def step(cells):
            volume[:, cells] = summed(k, cells)

        planes_in(ryb.at[now[0], k], k)
        each_chunk(step)

    def activate(cells):
        preact = summed(2, cells)
        normal = 0.5 * (1.0 + lax.erf(preact * 0.7071067811865476))
        density = jnp.exp(-0.5 * preact * preact) * 0.3989422804014327
        layer[:, cells] = (preact * normal).astype(BF)
        slope[0:160, cells] = (cot[:, cells].astype(F32) * (normal + preact * density)).astype(BF)

    def finish(cells):
        fgrad_raw[:, :, :, cells] = summed(2, cells).reshape(CH, 2, 4, 256).astype(BF)
        pltpu.make_async_copy(
            fgrad_raw.at[:, :, :, cells], fgrad_hbm.at[:, :, :, cells], store_sem.at[2]
        ).start()

    def flatten(raw, flat):
        flat[0:160] = raw[...].astype(F32).reshape(160, NX * NT).astype(BF)

    def unflatten(flat, raw):
        raw[...] = flat[...].astype(F32).reshape(CH, 2, 4, NX * NT).astype(BF)

    now = [0]

    def start_part(source, k):
        t = now[0]
        planes_out(source, k, sy.at[t, k])
        if t == 1:
            send_y(sy.at[t, k], ry.at[t, k], 12 * t + k)

    def y_part(k):
        t = now[0]
        arrive(ry.at[t, k], GY, 12 * t + k)
        y_forward(ry.at[t, k], sz.at[t, k])
        send_z(sz.at[t, k], rz.at[t, k], 12 * t + 3 + k)

    def z_part(k):
        t = now[0]
        arrive(rz.at[t, k], GZ, 12 * t + 3 + k)
        if t == 0:
            mix_forward(k)
        else:
            mix_back(k)
        send_z(szb.at[t, k], rzb.at[t, k], 12 * t + 6 + k)

    def back_part(k):
        t = now[0]
        arrive(rzb.at[t, k], GZ, 12 * t + 6 + k)
        y_back(rzb.at[t, k], syb.at[t, k])
        send_y(syb.at[t, k], ryb.at[t, k], 12 * t + 9 + k)

    def end_part(k):
        arrive(ryb.at[now[0], k], GY, 12 * now[0] + 9 + k)

    field[160:256] = jnp.zeros((96, NX * NT), BF)
    slope[160:256] = jnp.zeros((96, NX * NT), BF)
    got_field.wait()
    flatten(field_raw, field)
    for k in range(PARTS):
        got_plane[k].wait()
        start_part(field, k)
    pl.semaphore_wait(barrier, GY + GZ - 2)
    for k in range(PARTS):
        send_y(sy.at[0, k], ry.at[0, k], k)
    got_weight.wait()
    align_weights()
    small_tables()
    each_chunk(point_forward)
    got_yf.wait()
    y_part(0)
    got_zf.wait()
    got_spread.wait()
    got_gather.wait()
    got_mask.wait()
    got_zb.wait()
    got_yb.wait()
    got_cot.wait()
    flatten(cot_raw, cot)
    y_part(1)
    y_part(2)
    z_part(0)
    z_part(1)
    back_part(0)
    z_part(2)
    back_part(1)
    back_part(2)
    for k in range(2):
        end_part(k)
        add_part(k)
    end_part(2)
    planes_in(ryb.at[0, 2], 2)
    each_chunk(activate)
    put_layer = pltpu.make_async_copy(layer_raw, out_hbm, store_sem.at[0])
    now[0] = 1
    for k in range(PARTS):
        start_part(slope, k)
    unflatten(layer, layer_raw)
    put_layer.start()
    each_chunk(point_back)
    y_part(0)
    y_part(1)
    y_part(2)
    z_part(0)
    z_part(1)
    back_part(0)
    z_part(2)
    back_part(1)
    back_part(2)
    return_weights()
    put_wgrad = pltpu.make_async_copy(wgrad, wgrad_hbm, store_sem.at[1])
    put_wgrad.start()
    for k in range(2):
        end_part(k)
        add_part(k)
    end_part(2)
    planes_in(ryb.at[1, 2], 2)
    each_chunk(finish)
    for t in range(2):
        for k in range(PARTS):
            sent(sy.at[t, k], GY, 12 * t + k)
            sent(sz.at[t, k], GZ, 12 * t + 3 + k)
            sent(szb.at[t, k], GZ, 12 * t + 6 + k)
            sent(syb.at[t, k], GY, 12 * t + 9 + k)
    put_layer.wait()
    put_wgrad.wait()
    pltpu.make_async_copy(fgrad_raw, fgrad_hbm, store_sem.at[2]).wait()


def per_device(field, cotangent, spectral_weight, point_weight, channel_bias):
    cells = NX * NT
    whole = pl.BlockSpec(memory_space=pltpu.VMEM)
    anywhere = pl.BlockSpec(memory_space=pl.ANY)
    consts = constants()
    vm = pltpu.VMEM
    scratch = [
        vm((256, cells), BF),
        vm((160, cells), BF),
        vm((PAIRS, 7200), BF),
        vm((PARTS, 256, cells), BF),
        vm((512, 256), BF),
        vm((8 * LINES, 128), BF),
        vm((512, 384), BF),
        vm((1024, 128), BF),
        vm((2, 256, 512), BF),
        vm((2, 512, 256), BF),
        vm((2, 128, 128), F32),
        vm((256, cells), BF),
        vm((160, cells), BF),
        vm((PROWS, 7296), F32),
        vm((PARTS, 128, 512), F32),
        vm((PARTS, 128, 512), F32),
        vm((PARTS, 128, 512), F32),
        vm((PARTS, 128, 512), F32),
        vm((PROWS, 7296), F32),
        vm((PAIRS, 7200), F32),
        vm((160, cells), F32),
        vm((PARTS, 256, 256), BF),
        vm((PARTS, 128, 128), F32),
        vm((160, 160), BF),
        vm((160, 160), BF),
        vm((160, 128), F32),
        vm((CH, 2, 4, cells), BF),
        vm((CH, 2, 4, cells), BF),
        vm((CH, 2, 4, cells), BF),
        vm((CH, 2, 4, cells), BF),
        vm((2, PARTS, GY, SLAB, 128), BF),
        vm((2, PARTS, GY, SLAB, 128), BF),
        vm((2, PARTS, GZ, SLAB, 128), BF),
        vm((2, PARTS, GZ, SLAB, 128), BF),
        vm((2, PARTS, GZ, SLAB, 128), BF),
        vm((2, PARTS, GZ, SLAB, 128), BF),
        vm((2, PARTS, GY, SLAB, 128), BF),
        vm((2, PARTS, GY, SLAB, 128), BF),
        pltpu.SemaphoreType.DMA((13,)),
        pltpu.SemaphoreType.DMA((3,)),
        pltpu.SemaphoreType.DMA((24,)),
        pltpu.SemaphoreType.DMA((24,)),
    ]
    layer, fgrad, wgrad = pl.pallas_call(
        kernel,
        out_shape=(
            jax.ShapeDtypeStruct(field.shape, BF),
            jax.ShapeDtypeStruct(field.shape, BF),
            jax.ShapeDtypeStruct((PAIRS, 7200), F32),
        ),
        in_specs=[anywhere, anywhere, anywhere, whole, whole] + [anywhere] * len(consts),
        out_specs=(anywhere, anywhere, anywhere),
        scratch_shapes=scratch,
        compiler_params=pltpu.CompilerParams(
            collective_id=0, has_side_effects=True, vmem_limit_bytes=60 * 1024 * 1024
        ),
    )(field, cotangent, spectral_weight, point_weight, channel_bias.reshape(1, CH), *consts)
    return layer, fgrad, wgrad


def solution(mesh):
    return jax.shard_map(
        per_device,
        mesh=mesh,
        in_specs=(P(None, "gy", "gz", None), P(None, "gy", "gz", None), P("gz", "gy"), P(), P()),
        out_specs=(P(None, "gy", "gz", None), P(None, "gy", "gz", None), P("gz", "gy")),
        check_vma=False,
    )
```

```python
import functools

import jax
import jax.numpy as jnp
import ml_dtypes
import numpy as np
from jax import lax
from jax.experimental import pallas as pl
from jax.experimental.pallas import tpu as pltpu
from jax.sharding import PartitionSpec as P

MODES = 12
NX = 64
NY = 64
NZ = 64
NT = 32
CH = 20
GY = 32
GZ = 16
PAIRS = 36
PROWS = 40
SLAB = 8
PARTS = 3
LINES = 168
MESH = pl.DeviceIdType.MESH
BF = jnp.bfloat16
F32 = jnp.float32


def kept(slots, length):
    return np.where(slots < MODES, slots, length - 2 * MODES + slots)


def plane_constant():
    cell = np.arange(NX * NT)
    x, t = cell // NT, cell % NT
    out = np.zeros((GY, 3, 8, NX * NT))
    for d in range(GY):
        for k in range(3):
            for q3 in range(3):
                q = 9 * d + 3 * k + q3
                kx, kt = kept(np.array(q // MODES), NX), q % MODES
                angle = 2 * np.pi * ((kx * x % NX) / NX + (kt * t % NT) / NT)
                out[d, k, 2 * q3] = np.cos(angle)
                out[d, k, 2 * q3 + 1] = -np.sin(angle)
    return out.transpose(1, 0, 2, 3).reshape(PARTS, GY * SLAB, NX * NT)


def slot_frequency(length):
    g = np.arange(GZ)[:, None]
    return kept(3 * g // 2 + np.arange(2)[None, :], length)


def on_slabs(cosine, sine):
    rows, cols = cosine.shape
    two = np.stack([np.stack([cosine, sine], -1), np.stack([-sine, cosine], -1)], 2)
    full = np.einsum("rcab,uv->ruacvb", two.transpose(0, 1, 2, 3), np.eye(4))
    return full.reshape(rows * SLAB, cols * SLAB)


def y_constants():
    ky = slot_frequency(NY)
    y = 2 * np.arange(GY)[None, :] + np.arange(2)[:, None]
    angle = 2 * np.pi * (ky[None, :, :, None] * y[:, None, None, :] % NY) / NY
    near = angle.transpose(0, 2, 1, 3)
    forward = on_slabs(np.cos(near).reshape(-1, GY), np.sin(near).reshape(-1, GY))
    far = angle.transpose(0, 2, 3, 1)
    back = on_slabs(np.cos(far).reshape(-1, GZ), -np.sin(far).reshape(-1, GZ))
    return forward, back


def pair_slots(parity):
    p = np.arange(PAIRS) + 12 * parity
    return p // 24, p % 24


def z_constants():
    forward = np.zeros((2, 4, 2, LINES, GZ, 4, 2))
    back = np.zeros((2, 4, GZ, 4, 2, 2, LINES))
    for parity in range(2):
        kz = kept(pair_slots(parity)[1], NZ)
        for zl in range(4):
            angle = 2 * np.pi * (kz[:, None] * (4 * np.arange(GZ) + zl)[None, :] % NZ) / NZ
            c, s = np.cos(angle), np.sin(angle)
            for u in range(4):
                rows = slice(PROWS * u, PROWS * u + PAIRS) if u < 3 else slice(128, 128 + PAIRS)
                forward[parity, zl, 0, rows, :, u, 0] = c
                forward[parity, zl, 0, rows, :, u, 1] = s
                forward[parity, zl, 1, rows, :, u, 0] = -s
                forward[parity, zl, 1, rows, :, u, 1] = c
                back[parity, zl, :, u, 0, 0, rows] = c.T
                back[parity, zl, :, u, 0, 1, rows] = -s.T
                back[parity, zl, :, u, 1, 0, rows] = s.T
                back[parity, zl, :, u, 1, 1, rows] = c.T
    back = np.pad(back.reshape(2, 4 * GZ * SLAB, 2 * LINES), ((0, 0), (0, 0), (0, 384 - 2 * LINES)))
    return forward.reshape(2, 8 * LINES, GZ * SLAB), back


def mask_constant():
    lane = np.arange(128)
    out = np.zeros((2, 2, 128, 128))
    for parity in range(2):
        slot = pair_slots(parity)[0]
        for q3 in range(3):
            rows = slice(PROWS * q3, PROWS * q3 + PAIRS)
            match = (lane // 4 % 2)[None, :] == slot[:, None]
            out[parity, 0, rows] = match
            out[parity, 1, rows] = match & (lane // 32 == q3)[None, :]
    return out


def channel_constants():
    lane = np.arange(128)
    channel = np.concatenate([lane // 8, np.where(lane < 96, 16 + lane % 32 // 8, -1)])
    pair = np.arange(512)
    first = np.where(pair < CH * CH, pair // CH, -2)
    second = np.where(pair < CH * CH, pair % CH, -2)
    return channel[:, None] == first[None, :], channel[:, None] == second[None, :]


@functools.cache
def constants():
    half = lambda a: np.asarray(a, np.float32).astype(ml_dtypes.bfloat16)
    y_forward, y_back = y_constants()
    z_forward, z_back = z_constants()
    first, second = channel_constants()
    spread = np.stack([first, second])
    return (
        half(plane_constant()),
        half(y_forward),
        half(z_forward),
        half(z_back),
        half(y_back),
        half(spread),
        half(spread.transpose(0, 2, 1)),
        np.asarray(mask_constant(), np.float32),
    )


def dot(a, b):
    return jnp.dot(a, b, preferred_element_type=F32)


def dot_t(a, b):
    return lax.dot_general(a, b, (((1,), (1,)), ((), ())), preferred_element_type=F32)


def lanes(shape):
    return lax.broadcasted_iota(jnp.int32, shape, len(shape) - 1)


def kernel(
    field_hbm, cot_hbm, weight_hbm, point_ref, bias_ref,
    plane_hbm, yf_hbm, zf_hbm, zb_hbm, yb_hbm, spread_hbm, gather_hbm, mask_hbm,
    out_hbm, fgrad_hbm, wgrad_hbm,
    field, cot, weight, plane, yf, zf, zb, yb, spread, gather, mask,
    slope, layer, wf, w0, w1, u0, u1, wg, wgrad, volume, turned, scale, point_fwd, point_bwd, bias_col,
    field_raw, cot_raw, layer_raw, fgrad_raw,
    sy, ry, sz, rz, szb, rzb, syb, ryb, load_sem, store_sem, send_sem, recv_sem,
):
    j = lax.axis_index("gy")
    g = lax.axis_index("gz")
    parity = lax.rem(g, 2)

    barrier = pltpu.get_barrier_semaphore()

    def greet(axis, other):
        pl.semaphore_signal(barrier, inc=1, device_id={axis: other}, device_id_type=MESH)

    def greet_y():
        near = j // 16 * 16
        far = 16 - near
        z = lax.rem(j, 16)
        half = lax.rem(z + 8, 16)
        greet("gy", far + half)
        greet("gy", near + half)

        def one(i, carry):
            up = lax.rem(z + 8 - i, 16)
            down = lax.rem(z + 8 + i, 16)
            greet("gy", far + up)
            greet("gy", far + down)
            greet("gy", near + up)
            greet("gy", near + down)
            return carry

        lax.fori_loop(1, 8, one, 0)
        greet("gy", far + z)

    def greet_z():
        def one(i, carry):
            greet("gz", lax.rem(g + i, 16))
            return carry

        lax.fori_loop(1, 16, one, 0)

    greet_y()
    greet_z()

    def load(i, src, dst):
        copy = pltpu.make_async_copy(src, dst, load_sem.at[i])
        copy.start()
        return copy

    got_field = load(0, field_hbm, field_raw)
    got_plane = [load(1 + k, plane_hbm.at[k], plane.at[k]) for k in range(PARTS)]
    got_yf = load(4, yf_hbm, yf)
    got_weight = load(5, weight_hbm, weight)
    got_zf = load(6, zf_hbm.at[parity], zf)
    got_spread = load(7, spread_hbm, spread)
    got_gather = load(8, gather_hbm, gather)
    got_mask = load(9, mask_hbm.at[parity], mask)
    got_zb = load(10, zb_hbm.at[parity], zb)
    got_yb = load(11, yb_hbm, yb)
    got_cot = load(12, cot_hbm, cot_raw)

    def copy_to(src, dst, axis, me, other, which):
        pltpu.make_async_remote_copy(
            src_ref=src.at[other],
            dst_ref=dst.at[me],
            send_sem=send_sem.at[which],
            recv_sem=recv_sem.at[which],
            device_id={axis: other},
            device_id_type=MESH,
        ).start()

    def send_y(src, dst, which):
        near = j // 16 * 16
        far = 16 - near
        z = lax.rem(j, 16)
        half = lax.rem(z + 8, 16)
        copy_to(src, dst, "gy", j, near + half, which)
        copy_to(src, dst, "gy", j, far + half, which)

        def one(i, carry):
            up = lax.rem(z + 8 - i, 16)
            down = lax.rem(z + 8 + i, 16)
            copy_to(src, dst, "gy", j, far + up, which)
            copy_to(src, dst, "gy", j, far + down, which)
            copy_to(src, dst, "gy", j, near + up, which)
            copy_to(src, dst, "gy", j, near + down, which)
            return carry

        lax.fori_loop(1, 8, one, 0)
        copy_to(src, dst, "gy", j, far + z, which)
        dst[pl.ds(j, 1)] = src[pl.ds(j, 1)]

    def send_z(src, dst, which):
        for step in (12, 13, 11, 10, 14, 8, 9, 15, 4, 5, 3, 2, 6, 7, 1):
            copy_to(src, dst, "gz", g, lax.rem(g + step, 16), which)
        dst[pl.ds(g, 1)] = src[pl.ds(g, 1)]

    def arrive(dst, count, which):
        part = pl.ds(0, count - 1)
        pltpu.make_async_copy(dst.at[part], dst.at[part], recv_sem.at[which]).wait()

    def sent(src, count, which):
        part = pl.ds(0, count - 1)
        pltpu.make_async_copy(src.at[part], src.at[part], send_sem.at[which]).wait()

    zlane = lanes((1, 128)) % 4
    low_slot = lanes((1, 128)) // 4 % 2 == 0
    row3 = lax.broadcasted_iota(jnp.int32, (1, 8, 128), 1)
    lane3 = lanes((1, 8, 128))

    def planes_out(source, k, buffer):
        full = dot_t(plane[k], source[...])
        main = full[:, :128].reshape(GY, 8, 128)
        left = full[:, 128:].reshape(GY, 8, 128)
        extra = jnp.zeros_like(main)
        for q3 in range(3):
            moved = pltpu.roll(left, 6 - 2 * q3, 1)
            if q3:
                moved = pltpu.roll(moved, 32 * q3, 2)
            extra = jnp.where(lane3 // 32 == q3, moved, extra)
        buffer[...] = jnp.where(row3 >= 6, extra, main).astype(BF)

    def planes_in(buffer, k):
        block = buffer[...].astype(F32)
        left = jnp.zeros_like(block)
        for q3 in range(3):
            moved = pltpu.roll(block, 2 + 2 * q3, 1)
            if q3:
                moved = pltpu.roll(moved, 128 - 32 * q3, 2)
            left = jnp.where(row3 // 2 == q3, moved, left)
        turned[k, 0:128] = block.reshape(256, 128).T.astype(BF)
        turned[k, 128:160] = left.reshape(256, 128)[:, 0:32].T.astype(BF)

    def swap_slots(same_low, same_high, cross_low, cross_high):
        crossed = jnp.where(low_slot, pltpu.roll(cross_low, 124, 1), pltpu.roll(cross_high, 4, 1))
        return jnp.where(low_slot, same_low, same_high) + crossed

    def y_forward(buffer, target):
        block = buffer[...].reshape(256, 128)
        every = dot(yf[...], block)
        part = [every[128 * n : 128 * n + 128] for n in range(4)]
        target[...] = swap_slots(part[0], part[3], part[2], part[1]).reshape(GZ, SLAB, 128).astype(BF)

    def y_back(buffer, target):
        block = buffer[...].reshape(128, 128)
        every = dot(yb[...], block)
        part = [every[256 * n : 256 * n + 256] for n in range(4)]
        target[...] = swap_slots(part[0], part[3], part[1], part[2]).reshape(GY, SLAB, 128).astype(BF)

    def by_z(parts):
        low = jnp.where(zlane == 0, parts[0], parts[1])
        high = jnp.where(zlane == 2, parts[2], parts[3])
        return jnp.where(zlane < 2, low, high)

    def z_forward(buffer, factor):
        block = buffer[...].reshape(128, 128)
        step = 2 * LINES
        every = dot(zf[...], block)
        values = by_z([every[step * n : step * n + step] for n in range(4)]).reshape(2, LINES, 128)
        left = values[:, 128:]
        left = jnp.concatenate([left, left, left, jnp.zeros((2, 8, 128), F32)], axis=1)
        main = values[:, :128] * mask[0:1]
        left = left * mask[1:2]
        if factor is not None:
            main, left = main * factor[None], left * factor[None]
        return jnp.concatenate([main.reshape(256, 128).astype(BF), left.reshape(256, 128).astype(BF)], axis=1)

    def z_back(mixed, n, factor, target):
        values = dot(mixed, gather[n])
        main = values[:, :128].reshape(2, 128, 128) * mask[0:1]
        left = values[:, 128:].reshape(2, 128, 128) * mask[1:2]
        if factor is not None:
            main, left = main * factor[None], left * factor[None]
        left = left[:, 0:40] + left[:, 40:80] + left[:, 80:120]
        rows = jnp.concatenate([main, left], axis=1).reshape(2 * LINES, 128)
        rows = jnp.concatenate([rows, jnp.zeros((384 - 2 * LINES, 128), F32)], axis=0).astype(BF)
        every = dot(zb[...], rows)
        parts = [every[128 * n : 128 * n + 128] for n in range(4)]
        target[...] = by_z(parts).reshape(GZ, SLAB, 128).astype(BF)

    def mix_forward(k):
        spread_u = dot(z_forward(rz.at[0, k], None), spread[0])
        real_u, imag_u = spread_u[:128], spread_u[128:]
        u0[k] = real_u
        u1[k] = imag_u
        mixed_real = (real_u * w0[k] - imag_u * w1[k]).astype(BF)
        mixed_imag = (real_u * w1[k] + imag_u * w0[k]).astype(BF)
        z_back(jnp.concatenate([mixed_real, mixed_imag], axis=0), 1, scale[k], szb.at[0, k])

    def mix_back(k):
        spread_g = dot(z_forward(rz.at[1, k], scale[k]), spread[1])
        real_g, imag_g = spread_g[:128], spread_g[128:]
        mixed_real = (real_g * w0[k] + imag_g * w1[k]).astype(BF)
        mixed_imag = (imag_g * w0[k] - real_g * w1[k]).astype(BF)
        z_back(jnp.concatenate([mixed_real, mixed_imag], axis=0), 0, None, szb.at[1, k])
        w0[k] = u0[k] * real_g + u1[k] * imag_g
        w1[k] = u0[k] * imag_g - u1[k] * real_g

    def align_weights():
        wf[...] = jnp.zeros((PROWS, 7296), F32)
        wf[0:PAIRS, 0:7200] = weight[...].astype(F32)
        w0[...] = jnp.zeros((PARTS, 128, 512), F32)
        w1[...] = jnp.zeros((PARTS, 128, 512), F32)
        for q in range(9):
            for part, held in enumerate((w0, w1)):
                start = 800 * q + 400 * part
                first, shift = start // 128 * 128, start % 128
                piece = wf[:, first : first + 512]
                if shift:
                    piece = pltpu.roll(piece, 512 - shift, 1)
                top = PROWS * (q % 3)
                held[q // 3, top : top + PROWS] = piece

    def return_weights():
        wg[...] = jnp.zeros((PROWS, 7296), F32)
        for q in range(9):
            for part, held in enumerate((w0, w1)):
                start = 800 * q + 400 * part
                first, shift = start // 128 * 128, start % 128
                top = PROWS * (q % 3)
                piece = held[q // 3, top : top + PROWS]
                if shift:
                    piece = pltpu.roll(piece, shift, 1)
                wg[:, first : first + 512] = wg[:, first : first + 512] + piece
        wgrad[...] = wg[0:PAIRS, 0:7200]

    def small_tables():
        row = lax.broadcasted_iota(jnp.int32, (128, 128), 0)
        for k in range(PARTS):
            mode = 9 * j + 3 * k + (row >= 40).astype(jnp.int32) + (row >= 80).astype(jnp.int32)
            scale[k] = jnp.where(mode % MODES == 0, 1.0, 2.0) * (1.0 / (NX * NY * NZ * NT))
        copies = (lax.broadcasted_iota(jnp.int32, (160, CH), 0) // 8 == lanes((160, CH))).astype(F32)
        copies_half = copies.astype(BF)
        same_row = lax.broadcasted_iota(jnp.int32, (160, 160), 0) % 8 == lanes((160, 160)) % 8
        by_out = dot_t(copies_half, point_ref[...]).astype(BF)
        by_in = dot(copies_half, point_ref[...]).astype(BF)
        point_fwd[...] = jnp.where(same_row, dot_t(by_out, copies_half), 0.0).astype(BF)
        point_bwd[...] = jnp.where(same_row, dot_t(by_in, copies_half), 0.0).astype(BF)
        bias_col[...] = jnp.broadcast_to(jnp.sum(copies * bias_ref[...], axis=1, keepdims=True), (160, 128))

    def each_chunk(step):
        def one(n, carry):
            step(pl.ds(pl.multiple_of(n * 256, 256), 256))
            return carry

        lax.fori_loop(0, NX * NT // 256, one, 0)

    def point_forward(cells):
        volume[:, cells] = dot(point_fwd[...], field[0:160, cells]) + bias_col[:, 0:1]

    def point_back(cells):
        volume[:, cells] = dot(point_bwd[...], slope[0:160, cells])

    def summed(k, cells):
        return volume[:, cells] + dot(turned[k, 0:160], plane[k, :, cells])

    def add_part(k):
        def step(cells):
            volume[:, cells] = summed(k, cells)

        planes_in(ryb.at[now[0], k], k)
        for n in range(8):
            step(pl.ds(256 * n, 256))

    def activate(cells):
        preact = summed(2, cells)
        normal = 0.5 * (1.0 + lax.erf(preact * 0.7071067811865476))
        density = jnp.exp(-0.5 * preact * preact) * 0.3989422804014327
        layer[:, cells] = (preact * normal).astype(BF)
        slope[0:160, cells] = (cot[:, cells].astype(F32) * (normal + preact * density)).astype(BF)

    def finish(cells):
        fgrad_raw[:, :, :, cells] = summed(2, cells).reshape(CH, 2, 4, 256).astype(BF)
        pltpu.make_async_copy(
            fgrad_raw.at[:, :, :, cells], fgrad_hbm.at[:, :, :, cells], store_sem.at[2]
        ).start()

    def flatten(raw, flat):
        flat[0:160] = raw[...].astype(F32).reshape(160, NX * NT).astype(BF)

    def unflatten(flat, raw):
        raw[...] = flat[...].astype(F32).reshape(CH, 2, 4, NX * NT).astype(BF)

    now = [0]

    def start_part(source, k):
        t = now[0]
        planes_out(source, k, sy.at[t, k])
        if t == 1:
            send_y(sy.at[t, k], ry.at[t, k], 12 * t + k)

    def y_part(k):
        t = now[0]
        arrive(ry.at[t, k], GY, 12 * t + k)
        y_forward(ry.at[t, k], sz.at[t, k])
        send_z(sz.at[t, k], rz.at[t, k], 12 * t + 3 + k)

    def z_part(k):
        t = now[0]
        arrive(rz.at[t, k], GZ, 12 * t + 3 + k)
        if t == 0:
            mix_forward(k)
        else:
            mix_back(k)
        send_z(szb.at[t, k], rzb.at[t, k], 12 * t + 6 + k)

    def back_part(k):
        t = now[0]
        arrive(rzb.at[t, k], GZ, 12 * t + 6 + k)
        y_back(rzb.at[t, k], syb.at[t, k])
        send_y(syb.at[t, k], ryb.at[t, k], 12 * t + 9 + k)

    def end_part(k):
        arrive(ryb.at[now[0], k], GY, 12 * now[0] + 9 + k)

    field[160:256] = jnp.zeros((96, NX * NT), BF)
    slope[160:256] = jnp.zeros((96, NX * NT), BF)
    got_field.wait()
    flatten(field_raw, field)
    for k in range(PARTS):
        got_plane[k].wait()
        start_part(field, k)
    pl.semaphore_wait(barrier, GY + GZ - 2)
    for k in range(PARTS):
        send_y(sy.at[0, k], ry.at[0, k], k)
    got_weight.wait()
    align_weights()
    small_tables()
    each_chunk(point_forward)
    got_yf.wait()
    y_part(0)
    got_zf.wait()
    got_spread.wait()
    got_gather.wait()
    got_mask.wait()
    got_zb.wait()
    got_yb.wait()
    got_cot.wait()
    flatten(cot_raw, cot)
    y_part(1)
    y_part(2)
    z_part(0)
    z_part(1)
    back_part(0)
    z_part(2)
    back_part(1)
    back_part(2)
    for k in range(2):
        end_part(k)
        add_part(k)
    end_part(2)
    planes_in(ryb.at[0, 2], 2)
    for n in range(8):
        activate(pl.ds(256 * n, 256))
    put_layer = pltpu.make_async_copy(layer_raw, out_hbm, store_sem.at[0])
    now[0] = 1
    for k in range(PARTS):
        start_part(slope, k)
    unflatten(layer, layer_raw)
    put_layer.start()
    each_chunk(point_back)
    y_part(0)
    y_part(1)
    y_part(2)
    z_part(0)
    z_part(1)
    back_part(0)
    z_part(2)
    back_part(1)
    back_part(2)
    return_weights()
    put_wgrad = pltpu.make_async_copy(wgrad, wgrad_hbm, store_sem.at[1])
    put_wgrad.start()
    for t in range(2):
        for k in range(PARTS):
            sent(sy.at[t, k], GY, 12 * t + k)
            sent(sz.at[t, k], GZ, 12 * t + 3 + k)
            sent(szb.at[t, k], GZ, 12 * t + 6 + k)
            if t == 0:
                sent(syb.at[t, k], GY, 12 * t + 9 + k)
    put_layer.wait()
    put_wgrad.wait()
    for k in range(2):
        end_part(k)
        add_part(k)
    end_part(2)
    planes_in(ryb.at[1, 2], 2)
    for n in range(8):
        finish(pl.ds(256 * n, 256))
    for k in range(PARTS):
        sent(syb.at[1, k], GY, 21 + k)
    pltpu.make_async_copy(fgrad_raw, fgrad_hbm, store_sem.at[2]).wait()


def store_kernel(*refs):
    sources, targets, held, sem_in, sem_out = refs[:3], refs[3:6], refs[6:9], refs[9], refs[10]
    arriving, leaving = [], []
    for source, target, room in zip(sources, targets, held):
        pieces = [(4 * n, 4) for n in range(5)] if len(source.shape) == 4 else [(0, 8), (8, 8), (16, 8), (24, 12)]
        for first, count in pieces:
            rows = pl.ds(first, count)
            n = len(arriving)
            copy = pltpu.make_async_copy(source.at[rows], room.at[rows], sem_in.at[n])
            copy.start()
            arriving.append(copy)
            leaving.append(pltpu.make_async_copy(room.at[rows], target.at[rows], sem_out.at[n]))
    for copy, after in zip(arriving, leaving):
        copy.wait()
        after.start()
    for after in leaving:
        after.wait()


def store(*arrays):
    anywhere = pl.BlockSpec(memory_space=pl.ANY)
    return pl.pallas_call(
        store_kernel,
        out_shape=tuple(jax.ShapeDtypeStruct(a.shape, a.dtype) for a in arrays),
        in_specs=[anywhere] * 3,
        out_specs=(anywhere,) * 3,
        scratch_shapes=[pltpu.VMEM(a.shape, a.dtype) for a in arrays] + [pltpu.SemaphoreType.DMA((14,))] * 2,
        compiler_params=pltpu.CompilerParams(vmem_limit_bytes=60 * 1024 * 1024),
    )(*arrays)


def per_device(field, cotangent, spectral_weight, point_weight, channel_bias):
    cells = NX * NT
    whole = pl.BlockSpec(memory_space=pltpu.VMEM)
    anywhere = pl.BlockSpec(memory_space=pl.ANY)
    consts = constants()
    vm = pltpu.VMEM
    scratch = [
        vm((256, cells), BF),
        vm((160, cells), BF),
        vm((PAIRS, 7200), BF),
        vm((PARTS, 256, cells), BF),
        vm((512, 256), BF),
        vm((8 * LINES, 128), BF),
        vm((512, 384), BF),
        vm((1024, 128), BF),
        vm((2, 256, 512), BF),
        vm((2, 512, 256), BF),
        vm((2, 128, 128), F32),
        vm((256, cells), BF),
        vm((160, cells), BF),
        vm((PROWS, 7296), F32),
        vm((PARTS, 128, 512), F32),
        vm((PARTS, 128, 512), F32),
        vm((PARTS, 128, 512), F32),
        vm((PARTS, 128, 512), F32),
        vm((PROWS, 7296), F32),
        vm((PAIRS, 7200), F32),
        vm((160, cells), F32),
        vm((PARTS, 256, 256), BF),
        vm((PARTS, 128, 128), F32),
        vm((160, 160), BF),
        vm((160, 160), BF),
        vm((160, 128), F32),
        vm((CH, 2, 4, cells), BF),
        vm((CH, 2, 4, cells), BF),
        vm((CH, 2, 4, cells), BF),
        vm((CH, 2, 4, cells), BF),
        vm((2, PARTS, GY, SLAB, 128), BF),
        vm((2, PARTS, GY, SLAB, 128), BF),
        vm((2, PARTS, GZ, SLAB, 128), BF),
        vm((2, PARTS, GZ, SLAB, 128), BF),
        vm((2, PARTS, GZ, SLAB, 128), BF),
        vm((2, PARTS, GZ, SLAB, 128), BF),
        vm((2, PARTS, GY, SLAB, 128), BF),
        vm((2, PARTS, GY, SLAB, 128), BF),
        pltpu.SemaphoreType.DMA((13,)),
        pltpu.SemaphoreType.DMA((3,)),
        pltpu.SemaphoreType.DMA((24,)),
        pltpu.SemaphoreType.DMA((24,)),
    ]
    layer, fgrad, wgrad = pl.pallas_call(
        kernel,
        out_shape=(
            jax.ShapeDtypeStruct(field.shape, BF),
            jax.ShapeDtypeStruct(field.shape, BF),
            jax.ShapeDtypeStruct((PAIRS, 7200), F32),
        ),
        in_specs=[anywhere, anywhere, anywhere, whole, whole] + [anywhere] * len(consts),
        out_specs=(anywhere, anywhere, anywhere),
        scratch_shapes=scratch,
        compiler_params=pltpu.CompilerParams(
            collective_id=0, has_side_effects=True, vmem_limit_bytes=60 * 1024 * 1024
        ),
    )(field, cotangent, spectral_weight, point_weight, channel_bias.reshape(1, CH), *consts)
    return store(layer, fgrad, wgrad)


def solution(mesh):
    return jax.shard_map(
        per_device,
        mesh=mesh,
        in_specs=(P(None, "gy", "gz", None), P(None, "gy", "gz", None), P("gz", "gy"), P(), P()),
        out_specs=(P(None, "gy", "gz", None), P(None, "gy", "gz", None), P("gz", "gy")),
        check_vma=False,
    )
```
